256 devices in a mesh: dp: 32 (over y, x, core), tensor: 8 (over z).
Axes of the slice: x: 4, y: 4, z: 8, core: 2. Of those that a mesh axis runs over, the one named last changes fastest.
Arguments:
- tokens: bfloat16 [24576, 2560], P('dp', 'tensor'), may hold values from -6 to 6
- w_in: bfloat16 [2560, 5120], P(None, 'tensor'), may hold values from -0.125 to 0.125
- pre_act: bfloat16 [24576, 5120], P('dp', 'tensor'), may hold values from -5 to 5
- grad_hidden: bfloat16 [24576, 5120], P('dp', 'tensor'), may hold values from -3 to 3
- err_state: float32 [32, 2560, 5120], P('dp', None, 'tensor'), may hold values from -3072 to 3072
- q_init: float32 [5120, 64], P('tensor'), may hold values from -6 to 6
Outputs:
- grad_input: bfloat16 [24576, 2560], P('dp', 'tensor')
- q_factor: float32 [5120, 64], P('tensor')
The draws below stay inside these ranges and needn't reach their ends.
All inputs are finite; a program needn't handle non-finite values.
Results may differ from the reference program's by a relative error of at most 0.019.
Values may be sent and summed in bfloat16 or wider, within the bound.
A program may use at most 64 MiB of HBM per device.

```python
import math
import jax
import jax.numpy as jnp
from jax import lax

D = 2560
R = 64
TOK_DEV = 768
FF = 5120
GROUPS = 32
TOKENS = 24576
N_TENSOR = 8


def draw_err_state(key, part):
    key = jax.random.fold_in(key, 11)
    spread_scale = 0.3 * math.sqrt(TOK_DEV)
    limit_value = 4.0 * TOK_DEV
    drawn = spread_scale * jax.random.normal(key, (GROUPS, D, FF), jnp.float32)
    return jnp.clip(drawn, -limit_value, limit_value)


def steps_of(rng, extent, pieces, low, largest):
    def one(position, shards_of):
        draws = jax.random.uniform(jax.random.fold_in(jax.random.fold_in(rng, 6), position), (shards_of,), jnp.float32, low / len(pieces), largest / len(pieces))
        return jnp.repeat(jnp.exp(draws), extent[position] // shards_of).reshape((-1,) + (1,) * (len(extent) - position - 1))

    factor_of = one(*pieces[0])
    for cut in pieces[1:]:
        factor_of = factor_of * one(*cut)
    return factor_of


def centred(key, extent, spread, most, cuts=(), kind=jnp.bfloat16):
    level = steps_of(key, extent, cuts, -0.22, 0.18) if cuts else 1.0
    entries = jax.random.normal(key, extent, jnp.float32) * spread * level
    return jnp.minimum(jnp.maximum(entries, -most), most).astype(kind)


def setup_inputs(seed: int = 0) -> dict:
    keys = jax.random.split(jax.random.key(seed), 7)
    tokens = centred(keys[0], (TOKENS, D), 1.0, 6.0, ((0, 32), (1, 8)))
    w_in = centred(keys[1], (D, FF), D ** -0.5, 0.125, ((1, 8),))
    pre_act = centred(keys[2], (TOKENS, FF), 1.0, 5.0, ((0, 32), (1, 8)))
    grad_hidden = centred(keys[3], (TOKENS, FF), 0.5, 3.0, ((0, 32), (1, 8)))
    err_state = draw_err_state(jax.random.fold_in(keys[6], 71), 0)
    q_init = centred(keys[5], (FF, R), 1.0, 6.0, ((0, 8),), jnp.float32)
    return dict(tokens=tokens, w_in=w_in, pre_act=pre_act, grad_hidden=grad_hidden, err_state=err_state, q_init=q_init)


slope_coeff = 0.7978845608

def gelu_slope(argument):
    inside = slope_coeff * (argument + 0.044715 * argument * argument * argument)
    tangent = jnp.tanh(inside)
    return 0.5 * (1.0 + tangent) + 0.5 * argument * (1.0 - tangent * tangent) * slope_coeff * (1.0 + 0.134145 * argument * argument)

def orthonormal(p_total):
    highest = lax.Precision.HIGHEST
    p_gram = jnp.dot(p_total.T, p_total, precision=highest)
    factor_low = jnp.linalg.cholesky(p_gram)
    return jax.scipy.linalg.solve_triangular(factor_low, p_total.T, lower=True).T

def reference(tokens, w_in, pre_act, grad_hidden, err_state, q_init):
    highest = lax.Precision.HIGHEST
    slopes = gelu_slope(pre_act.astype(jnp.float32))
    pre_grad = (grad_hidden.astype(jnp.float32) * slopes).astype(jnp.bfloat16)
    shard_cols = FF // N_TENSOR
    summed = jnp.zeros((tokens.shape[0], D), jnp.float32)
    for column_block in range(N_TENSOR):
        lo_col = column_block * shard_cols
        blocked = jnp.dot(pre_grad[:, lo_col:lo_col + shard_cols].astype(jnp.float32), w_in[:, lo_col:lo_col + shard_cols].T.astype(jnp.float32), preferred_element_type=jnp.float32)
        blocked = lax.optimization_barrier(blocked.astype(jnp.bfloat16))
        summed = summed + blocked.astype(jnp.float32)
    grad_input = summed.astype(jnp.bfloat16)
    pre_wide = pre_grad.astype(jnp.float32)
    token_wide = tokens.astype(jnp.float32)
    err_total = jnp.sum(err_state, axis=0)
    hidden_mix = jnp.dot(pre_wide, q_init, precision=highest)
    p_total = jnp.dot(token_wide.T, hidden_mix, precision=highest) + jnp.dot(err_total, q_init, precision=highest)
    p_ortho = orthonormal(p_total)
    token_proj = jnp.dot(token_wide, p_ortho, precision=highest)
    q_total = jnp.dot(pre_wide.T, token_proj, precision=highest) + jnp.dot(err_total.T, p_ortho, precision=highest)
    return (grad_input, q_total / GROUPS)
```

```python
import jax
import jax.numpy as jnp
from jax import lax
from jax.experimental import pallas as pl
from jax.experimental.pallas import tpu as pltpu
from jax.sharding import PartitionSpec as P

highest = lax.Precision.HIGHEST
slope_coeff = 0.7978845608
MESH = pl.DeviceIdType.MESH
F32, BF16 = jnp.float32, jnp.bfloat16
NX, NY, NZ = 4, 4, 8
R, TOK, FEAT, HID = 64, 768, 320, 640
NN = (((1,), (0,)), ((), ()))
NT = (((1,), (1,)), ((), ()))


def gelu_slope(argument):
    inside = slope_coeff * (argument + 0.044715 * argument * argument * argument)
    tangent = jnp.tanh(inside)
    return 0.5 * (1.0 + tangent) + 0.5 * argument * (1.0 - tangent * tangent) * slope_coeff * (
        1.0 + 0.134145 * argument * argument
    )


def halves(value):
    high = value.astype(BF16)
    return high, (value - high.astype(F32)).astype(BF16)


def dot(left, right, dims):
    return lax.dot_general(left, right, dims, preferred_element_type=F32)


def dot_wide(left, right, dims):
    rows = left.shape[0]
    both = dot(jnp.concatenate(halves(left), axis=0), right, dims)
    return both[:rows] + both[rows:]


def dot_wide2(left, right, dims):
    high, low = halves(right)
    return dot_wide(left, high, dims) + dot(left.astype(BF16), low, dims)


def inverse_factor(gram, work):
    row_id = lax.broadcasted_iota(jnp.int32, (R, R), 0)
    col_id = lax.broadcasted_iota(jnp.int32, (R, R), 1)
    eye = (row_id == col_id).astype(F32)
    work[...] = jnp.concatenate([gram, eye], axis=1)
    lane = lax.broadcasted_iota(jnp.int32, (1, 2 * R), 1)
    below = lax.broadcasted_iota(jnp.int32, (R, 1), 0)

    def step(k, carry):
        row = work[pl.ds(k, 1), :]
        here = lane == k
        pivot = jnp.sum(jnp.where(here, row, 0.0), axis=1, keepdims=True)
        whole = work[...]
        column = jnp.sum(jnp.where(here, whole, 0.0), axis=1, keepdims=True)
        ratio = jnp.where(below > k, column / pivot, 0.0)
        work[...] = whole - ratio * row
        return carry

    lax.fori_loop(0, R, step, 0)
    diag = jnp.sum(work[:, :R] * eye, axis=1, keepdims=True)
    return work[:, R:] * lax.rsqrt(diag)


def chain_kernel(
    xt, g, e, qt, out,
    h_part, h_rs, h_ag, z_part, z_rs, z_ag,
    px_part, px_c, px_x, px_y, px_row, pt,
    pe_part, pe_c, pe_x, pe_z, pf,
    y_part, y_c, y_x, y_y, y_f, work,
    s_z, r_z, s_x, r_x, s_y, r_y, s_c, r_c,
):
    dp, z = lax.axis_index("dp"), lax.axis_index("tensor")
    c, x, y = lax.rem(dp, 2), lax.rem(dp // 2, NX), dp // (2 * NX)
    o = 1 - c

    def at(yy, xx, cc, zz):
        return ((yy * NX + xx) * 2 + cc, zz)

    axes = {
        "z": (NZ, z, lambda j: at(y, x, c, j), s_z, r_z),
        "x": (NX, x, lambda j: at(y, j, c, z), s_x, r_x),
        "y": (NY, y, lambda j: at(j, x, c, z), s_y, r_y),
    }
    sent = []

    def start(axis, phase, src, dst):
        n, me, dev, ss, rs = axes[axis]
        for k in range(1, n):
            j = lax.rem(me + k, n)
            cp = pltpu.make_async_remote_copy(
                src_ref=src(j), dst_ref=dst(me), send_sem=ss.at[phase, k], recv_sem=rs.at[phase, me],
                device_id=dev(j), device_id_type=MESH)
            cp.start()
            sent.append(cp)

    def finish(axis, phase, dst):
        n, me, dev, ss, rs = axes[axis]
        for k in range(1, n):
            j = lax.rem(me + k, n)
            pltpu.make_async_remote_copy(
                src_ref=dst(j), dst_ref=dst(j), send_sem=ss.at[phase, k], recv_sem=rs.at[phase, j],
                device_id=dev(j), device_id_type=MESH).wait_recv()

    def swap(phase, src, dst):
        cp = pltpu.make_async_remote_copy(
            src_ref=src, dst_ref=dst, send_sem=s_c.at[phase], recv_sem=r_c.at[phase],
            device_id=at(y, x, o, z), device_id_type=MESH)
        cp.start()
        sent.append(cp)

    def swapped(phase, dst):
        pltpu.make_async_remote_copy(
            src_ref=dst, dst_ref=dst, send_sem=s_c.at[phase], recv_sem=r_c.at[phase],
            device_id=at(y, x, o, z), device_id_type=MESH).wait_recv()

    barrier = pltpu.get_barrier_semaphore()
    for axis in "zxy":
        n, me, dev = axes[axis][:3]
        for k in range(1, n):
            pl.semaphore_signal(barrier, inc=1, device_id=dev(lax.rem(me + k, n)), device_id_type=MESH)
    pl.semaphore_signal(barrier, inc=1, device_id=at(y, x, o, z), device_id_type=MESH)

    h_part[...] = dot_wide(qt[...], g[...], NT).reshape(NZ, 8, TOK)
    pl.semaphore_wait(barrier, 14)
    start("z", 0, lambda j: h_part.at[j], lambda i: h_rs.at[i])
    h_rs[z] = h_part[z]

    def error_rows(t, carry):
        rows = e[pl.ds(pl.multiple_of(t * FEAT, FEAT), FEAT), :]
        pe_part[:, :, t] = dot_wide2(qt[...], rows, NT).reshape(2, NX, 8, FEAT)
        return carry

    lax.fori_loop(0, NZ, error_rows, 0)
    swap(0, pe_part.at[o], pe_c)

    finish("z", 0, lambda i: h_rs.at[i])
    h_ag[z] = jnp.sum(h_rs[...], axis=0)
    start("z", 1, lambda j: h_ag.at[z], lambda i: h_ag.at[i])

    swapped(0, pe_c)
    pe_c[...] += pe_part[c]
    start("x", 0, lambda j: pe_c.at[j], lambda i: pe_x.at[i])
    pe_x[x] = pe_c[x]

    finish("z", 1, lambda i: h_ag.at[i])
    px_part[...] = dot_wide(h_ag[...].reshape(R, TOK), xt[...], NT).reshape(2, NX, 8, FEAT)
    swap(1, px_part.at[o], px_c)

    finish("x", 0, lambda i: pe_x.at[i])
    pe_x[x] = pe_x[0] + pe_x[1] + pe_x[2] + pe_x[3]
    start("z", 2, lambda j: pe_x.at[x, j], lambda i: pe_z.at[i])
    pe_z[z] = pe_x[x, z]

    swapped(1, px_c)
    px_c[...] += px_part[c]
    start("x", 1, lambda j: px_c.at[j], lambda i: px_x.at[i])
    px_x[x] = px_c[x]
    finish("x", 1, lambda i: px_x.at[i])
    finish("z", 2, lambda i: pe_z.at[i])
    px_y[y] = jnp.sum(px_x[...], axis=0) + jnp.sum(pe_z[...], axis=0)
    start("y", 0, lambda j: px_y.at[y], lambda i: px_y.at[i])
    finish("y", 0, lambda i: px_y.at[i])
    p_row = jnp.sum(px_y[...], axis=0)
    pt[c, x] = p_row
    pf[c, x, z] = p_row
    start("x", 2, lambda j: pt.at[c, x], lambda i: pt.at[c, i])
    start("z", 3, lambda j: pf.at[c, x, z], lambda i: pf.at[c, x, i])
    finish("x", 2, lambda i: pt.at[c, i])
    swap(2, pt.at[c], pt.at[c])
    swapped(2, pt.at[o])

    z_part[...] = dot_wide(pt[...].reshape(R, FEAT), xt[...], NN).reshape(NZ, 8, TOK)
    start("z", 4, lambda j: z_part.at[j], lambda i: z_rs.at[i])
    z_rs[z] = z_part[z]

    finish("z", 3, lambda i: pf.at[c, x, i])
    start("x", 3, lambda j: pf.at[c, x], lambda i: pf.at[c, i])

    finish("z", 4, lambda i: z_rs.at[i])
    z_ag[z] = jnp.sum(z_rs[...], axis=0)
    start("z", 5, lambda j: z_ag.at[z], lambda i: z_ag.at[i])

    finish("x", 3, lambda i: pf.at[c, i])
    swap(3, pf.at[c], pf.at[c])
    swapped(3, pf.at[o])

    def features(t, carry):
        gram, total = carry
        block = pf[:, :, t].reshape(R, FEAT)
        rows = e[pl.ds(pl.multiple_of(t * FEAT, FEAT), FEAT), :]
        gram += lax.dot_general(block, block, NT, precision=highest, preferred_element_type=F32)
        return gram, total + dot_wide2(block, rows, NN)

    gram, y_err = lax.fori_loop(0, NZ, features, (jnp.zeros((R, R), F32), jnp.zeros((R, HID), F32)))

    finish("z", 5, lambda i: z_ag.at[i])
    y_part[...] = (y_err + dot_wide(z_ag[...].reshape(R, TOK), g[...], NN)).reshape(2, NX, 8, HID)
    swap(4, y_part.at[o], y_c)
    inverse = inverse_factor(gram, work)
    swapped(4, y_c)
    y_c[...] += y_part[c]
    start("x", 4, lambda j: y_c.at[j], lambda i: y_x.at[i])
    y_x[x] = y_c[x]
    finish("x", 4, lambda i: y_x.at[i])
    y_y[y] = jnp.sum(y_x[...], axis=0)
    start("y", 1, lambda j: y_y.at[y], lambda i: y_y.at[i])
    finish("y", 1, lambda i: y_y.at[i])
    y_f[c, x] = jnp.sum(y_y[...], axis=0)
    start("x", 5, lambda j: y_f.at[c, x], lambda i: y_f.at[c, i])
    finish("x", 5, lambda i: y_f.at[c, i])
    swap(5, y_f.at[c], y_f.at[c])
    swapped(5, y_f.at[o])
    out[...] = lax.dot_general(
        inverse, y_f[...].reshape(R, HID), NN, precision=highest, preferred_element_type=F32
    ) * (1.0 / (NX * NY * 2))
    for cp in sent:
        cp.wait_send()


def chain(xt, g, e, qt):
    vm = lambda *shape: pltpu.VMEM(shape, F32)
    dma = pltpu.SemaphoreType.DMA
    spec = pl.BlockSpec(memory_space=pltpu.VMEM)
    return pl.pallas_call(
        chain_kernel,
        out_shape=jax.ShapeDtypeStruct((R, HID), F32),
        in_specs=[spec] * 4,
        out_specs=spec,
        scratch_shapes=[vm(NZ, 8, TOK)] * 6
        + [vm(2, NX, 8, FEAT), vm(NX, 8, FEAT), vm(NX, 8, FEAT), vm(NY, 8, FEAT), vm(8, FEAT), vm(2, NX, 8, FEAT)]
        + [vm(2, NX, NZ, 8, FEAT), vm(NX, NZ, 8, FEAT), vm(NX, NZ, 8, FEAT), vm(NZ, 8, FEAT), vm(2, NX, NZ, 8, FEAT)]
        + [vm(2, NX, 8, HID), vm(NX, 8, HID), vm(NX, 8, HID), vm(NY, 8, HID), vm(2, NX, 8, HID), vm(R, 2 * R)]
        + [dma((6, NZ)), dma((6, NZ)), dma((6, NX)), dma((6, NX)), dma((2, NY)), dma((2, NY)), dma((6,)), dma((6,))],
        compiler_params=pltpu.CompilerParams(
            collective_id=0, has_side_effects=True, vmem_limit_bytes=48 << 20),
        cost_estimate=pl.CostEstimate(flops=10**9, bytes_accessed=100 * 10**6, transcendentals=0),
        name="chain",
    )(xt, g, e, qt)


def local(tokens, w_in, pre_act, grad_hidden, err_state, q_init):
    slopes = gelu_slope(pre_act.astype(F32))
    pre_grad = (grad_hidden.astype(F32) * slopes).astype(BF16)
    partial_value = dot(w_in, pre_grad, NT)
    grad_input = lax.psum_scatter(partial_value.astype(BF16), "tensor", scatter_dimension=0, tiled=True)
    q_factor = chain(tokens.T, pre_grad, err_state[0], q_init.T)
    return (grad_input.T, q_factor.T)


def solution(mesh):
    return jax.shard_map(
        local,
        mesh=mesh,
        in_specs=(
            P("dp", "tensor"),
            P(None, "tensor"),
            P("dp", "tensor"),
            P("dp", "tensor"),
            P("dp", None, "tensor"),
            P("tensor", None),
        ),
        out_specs=(P("dp", "tensor"), P("tensor", None)),
        check_vma=False,
    )
```

```python
import jax
import jax.numpy as jnp
from jax import lax
from jax.experimental import pallas as pl
from jax.experimental.pallas import tpu as pltpu
from jax.sharding import PartitionSpec as P

highest = lax.Precision.HIGHEST
slope_coeff = 0.7978845608
MESH = pl.DeviceIdType.MESH
F32, BF16 = jnp.float32, jnp.bfloat16
NX, NY, NZ = 4, 4, 8
R, TOK, FEAT, HID = 64, 768, 320, 640
NCH = 2
HALF = FEAT // 2
CHUNK = HALF // NCH
HOPS = (4, 3, 3, 2, 2, 1, 1)
NN = (((1,), (0,)), ((), ()))
NT = (((1,), (1,)), ((), ()))


def gelu_slope(argument):
    square = argument * argument
    tangent = jnp.tanh(argument * (slope_coeff + (slope_coeff * 0.044715) * square))
    linear = argument * (slope_coeff + (slope_coeff * 0.134145) * square)
    return 0.5 * (1.0 + tangent) * (1.0 + (1.0 - tangent) * linear)


def halves(value):
    high = value.astype(BF16)
    return high, (value - high.astype(F32)).astype(BF16)


def dot(left, right, dims):
    return lax.dot_general(left, right, dims, preferred_element_type=F32)


def dot_wide(left, right, dims):
    rows = left.shape[0]
    both = dot(jnp.concatenate(halves(left), axis=0), right, dims)
    return both[:rows] + both[rows:]


def dot_wide2(left, right, dims):
    high, low = halves(right)
    return dot_wide(left, high, dims) + dot(left.astype(BF16), low, dims)


def pair_rows(value):
    n = value.shape[-1] // 2
    return jnp.concatenate([value[..., :n], value[..., n:]], axis=-2)


def unpair_rows(value):
    return jnp.concatenate([value[..., :8, :], value[..., 8:, :]], axis=-1)


def eliminate(work, first, last):
    whole = work[...]
    below = lax.broadcasted_iota(jnp.int32, (R, 1), 0)
    for k in range(first, last):
        row = whole[k:k + 1, :]
        column = whole[:, k:k + 1]
        ratio = jnp.where(below > k, column / whole[k:k + 1, k:k + 1], 0.0)
        whole = whole - ratio * row
    work[...] = whole


def kernel(
    pre_hbm, gh_hbm, qt_hbm, w_hbm, e_hbm, xt_hbm, q_out, gi_out,
    pre, gh, qt, w, e, xt, g, part, ring,
    h_part, h_rs, h_ag, z_part, z_rs, z_ag,
    px_part, px_c, px_x, px_y, pt,
    pe_part, pe_c, pe_x, pe_z, pf,
    y_part, y_c, y_x, y_y, y_f, y_err, work,
    s_z, r_z, s_x, r_x, s_y, r_y, s_c, r_c, s_g, r_g, s_in,
):
    dp, z = lax.axis_index("dp"), lax.axis_index("tensor")
    c, x, y = lax.rem(dp, 2), lax.rem(dp // 2, NX), dp // (2 * NX)
    o = 1 - c

    def at(yy, xx, cc, zz):
        return ((yy * NX + xx) * 2 + cc, zz)

    axes = {
        "z": (NZ, z, lambda j: at(y, x, c, j), s_z, r_z),
        "x": (NX, x, lambda j: at(y, j, c, z), s_x, r_x),
        "y": (NY, y, lambda j: at(j, x, c, z), s_y, r_y),
    }
    sent = []

    def remote(src, dst, ss, rs, dev):
        return pltpu.make_async_remote_copy(
            src_ref=src, dst_ref=dst, send_sem=ss, recv_sem=rs, device_id=dev, device_id_type=MESH)

    def push(src, dst, ss, rs, dev):
        cp = remote(src, dst, ss, rs, dev)
        cp.start()
        sent.append(cp)

    def start(axis, phase, src, dst):
        n, me, dev, ss, rs = axes[axis]
        for k in range(1, n):
            j = lax.rem(me + k, n)
            push(src(j), dst(me), ss.at[phase, k], rs.at[phase, me], dev(j))

    def finish(axis, phase, dst):
        n, me, dev, ss, rs = axes[axis]
        for k in range(1, n):
            j = lax.rem(me + k, n)
            remote(dst(j), dst(j), ss.at[phase, k], rs.at[phase, j], dev(j)).wait_recv()

    def swap(phase, src, dst):
        push(src, dst, s_c.at[phase], r_c.at[phase], at(y, x, o, z))

    def swapped(phase, dst):
        remote(dst, dst, s_c.at[phase], r_c.at[phase], at(y, x, o, z)).wait_recv()

    def shifted(direction, hops):
        return lax.rem(z + (hops if direction == 0 else NZ - hops), NZ)

    def piece(direction, m, ch):
        half = (direction + m) % 2
        return pl.ds(half * HALF + ch * CHUNK, CHUNK)

    def ring_send(direction, m, ch, src):
        push(src, ring.at[direction, m, ch], s_g.at[direction, m, ch], r_g.at[direction, m, ch],
             at(y, x, c, shifted(direction, 1)))

    def ring_first(direction, m):
        for ch in range(NCH):
            ring_send(direction, m, ch, part.at[shifted(direction, HOPS[m]), piece(direction, m, ch)])

    def ring_wait(direction, m, ch):
        slot = ring.at[direction, m, ch]
        remote(slot, slot, s_g.at[direction, m, ch], r_g.at[direction, m, ch],
               at(y, x, c, shifted(direction, 1))).wait_recv()

    def ring_event(m, ch):
        for direction in range(2):
            ring_wait(direction, m, ch)
            if m < 5:
                own = part[shifted(direction, HOPS[m + 2]), piece(direction, m, ch)]
                ring[direction, m, ch] = (ring[direction, m, ch].astype(F32) + own.astype(F32)).astype(BF16)
                ring_send(direction, m + 2, ch, ring.at[direction, m, ch])

    events = [(m, ch) for m in range(7) for ch in range(NCH)]

    def pump(count):
        for _ in range(count):
            if events:
                ring_event(*events.pop(0))

    def product(t):
        rows = w[pl.ds(pl.multiple_of(t * FEAT, FEAT), FEAT), :]
        part[t] = dot(rows, g[...], NT).astype(BF16)

    loads = [
        pltpu.make_async_copy(src, dst, s_in.at[i])
        for i, (src, dst) in enumerate(
            [(pre_hbm, pre), (gh_hbm, gh), (qt_hbm, qt), (w_hbm, w), (e_hbm, e), (xt_hbm, xt)])
    ]
    for cp in loads:
        cp.start()
    barrier = pltpu.get_barrier_semaphore()
    for axis in "zxy":
        n, me, dev = axes[axis][:3]
        for k in range(1, n):
            pl.semaphore_signal(barrier, inc=1, device_id=dev(lax.rem(me + k, n)), device_id_type=MESH)
    pl.semaphore_signal(barrier, inc=1, device_id=at(y, x, o, z), device_id_type=MESH)

    loads[0].wait()
    loads[1].wait()

    def activate(i, carry):
        rows = pl.ds(pl.multiple_of(i * 64, 64), 64)
        g[rows, :] = (gh[rows, :].astype(F32) * gelu_slope(pre[rows, :].astype(F32))).astype(BF16)
        return carry

    lax.fori_loop(0, TOK // 64, activate, 0)
    loads[2].wait()
    h_part[...] = pair_rows(dot_wide(qt[...], g[...], NT).reshape(NZ, 8, TOK)).astype(BF16)
    pl.semaphore_wait(barrier, 14)
    start("z", 0, lambda j: h_part.at[j], lambda i: h_rs.at[i])
    h_rs[z] = h_part[z]

    loads[3].wait()
    product(shifted(0, 4))
    ring_first(0, 0)
    ring_first(1, 0)
    product(shifted(0, 3))
    ring_first(0, 1)
    product(shifted(1, 3))
    ring_first(1, 1)

    loads[4].wait()

    def error_rows(t, carry):
        rows = e[pl.ds(pl.multiple_of(t * FEAT, FEAT), FEAT), :]
        pe_part[:, :, t] = dot_wide2(qt[...], rows, NT).reshape(2, NX, 8, FEAT)
        return carry

    lax.fori_loop(0, NZ, error_rows, 0)
    swap(0, pe_part.at[o], pe_c)

    finish("z", 0, lambda i: h_rs.at[i])
    h_ag[z] = jnp.sum(h_rs[...].astype(F32), axis=0).astype(BF16)
    start("z", 1, lambda j: h_ag.at[z], lambda i: h_ag.at[i])

    product(shifted(0, 2))
    product(shifted(1, 2))
    swapped(0, pe_c)
    pe_c[...] += pe_part[c]
    start("x", 0, lambda j: pe_c.at[j], lambda i: pe_x.at[i])
    pe_x[x] = pe_c[x]
    product(shifted(0, 1))
    product(shifted(1, 1))
    product(z)
    pump(2)

    loads[5].wait()
    finish("z", 1, lambda i: h_ag.at[i])
    h_all = unpair_rows(h_ag[...].astype(F32)).reshape(R, TOK).astype(BF16)
    px_part[...] = dot(h_all, xt[...], NT).reshape(2, NX, 8, FEAT)
    swap(1, px_part.at[o], px_c)

    finish("x", 0, lambda i: pe_x.at[i])
    pe_x[x] = pe_x[0] + pe_x[1] + pe_x[2] + pe_x[3]
    start("z", 2, lambda j: pe_x.at[x, j], lambda i: pe_z.at[i])
    pe_z[z] = pe_x[x, z]

    swapped(1, px_c)
    px_c[...] += px_part[c]
    start("x", 1, lambda j: px_c.at[j], lambda i: px_x.at[i])
    px_x[x] = px_c[x]
    pump(1)
    finish("x", 1, lambda i: px_x.at[i])
    finish("z", 2, lambda i: pe_z.at[i])
    px_y[y] = jnp.sum(px_x[...], axis=0) + jnp.sum(pe_z[...], axis=0)
    start("y", 0, lambda j: px_y.at[y], lambda i: px_y.at[i])
    pump(1)
    finish("y", 0, lambda i: px_y.at[i])
    p_row = jnp.sum(px_y[...], axis=0)
    pt[c, x] = p_row
    pf[c, x, z] = p_row
    start("x", 2, lambda j: pt.at[c, x], lambda i: pt.at[c, i])
    start("z", 3, lambda j: pf.at[c, x, z], lambda i: pf.at[c, x, i])
    pump(1)
    finish("x", 2, lambda i: pt.at[c, i])
    swap(2, pt.at[c], pt.at[c])
    swapped(2, pt.at[o])

    z_sum = dot_wide(pt[...].reshape(R, FEAT), xt[...], NN).reshape(NZ, 8, TOK)
    z_part[...] = pair_rows(z_sum).astype(BF16)
    start("z", 4, lambda j: z_part.at[j], lambda i: z_rs.at[i])
    z_rs[z] = z_part[z]

    finish("z", 3, lambda i: pf.at[c, x, i])
    start("x", 3, lambda j: pf.at[c, x], lambda i: pf.at[c, i])
    pump(2)

    finish("z", 4, lambda i: z_rs.at[i])
    z_ag[z] = jnp.sum(z_rs[...].astype(F32), axis=0).astype(BF16)
    start("z", 5, lambda j: z_ag.at[z], lambda i: z_ag.at[i])

    finish("x", 3, lambda i: pf.at[c, i])
    swap(3, pf.at[c], pf.at[c])
    pump(1)
    swapped(3, pf.at[o])

    def features(t, gram):
        block = pf[:, :, t].reshape(R, FEAT)
        rows = e[pl.ds(pl.multiple_of(t * FEAT, FEAT), FEAT), :]
        y_err[...] += dot_wide2(block, rows, NN)
        return gram + lax.dot_general(block, block, NT, precision=highest, preferred_element_type=F32)

    y_err[...] = jnp.zeros_like(y_err)
    gram = lax.fori_loop(0, NZ, features, jnp.zeros((R, R), F32))
    eye = (lax.broadcasted_iota(jnp.int32, (R, R), 0) == lax.broadcasted_iota(jnp.int32, (R, R), 1)).astype(F32)
    work[...] = jnp.concatenate([gram, eye], axis=1)

    pump(1)
    finish("z", 5, lambda i: z_ag.at[i])
    z_all = unpair_rows(z_ag[...].astype(F32)).reshape(R, TOK).astype(BF16)
    y_part[...] = (y_err[...] + dot(z_all, g[...], NN)).reshape(2, NX, 8, HID)
    swap(4, y_part.at[o], y_c)
    eliminate(work, 0, 8)
    swapped(4, y_c)
    y_c[...] += y_part[c]
    start("x", 4, lambda j: y_c.at[j], lambda i: y_x.at[i])
    y_x[x] = y_c[x]
    pump(1)
    eliminate(work, 8, 24)
    finish("x", 4, lambda i: y_x.at[i])
    y_y[y] = jnp.sum(y_x[...], axis=0)
    start("y", 1, lambda j: y_y.at[y], lambda i: y_y.at[i])
    pump(1)
    eliminate(work, 24, 40)
    finish("y", 1, lambda i: y_y.at[i])
    y_f[c, x] = jnp.sum(y_y[...], axis=0)
    start("x", 5, lambda j: y_f.at[c, x], lambda i: y_f.at[c, i])
    pump(1)
    eliminate(work, 40, 56)
    finish("x", 5, lambda i: y_f.at[c, i])
    swap(5, y_f.at[c], y_f.at[c])
    eliminate(work, 56, 64)
    diag = jnp.sum(work[:, :R] * eye, axis=1, keepdims=True)
    inverse = work[:, R:] * (lax.rsqrt(diag) * (1.0 / (NX * NY * 2)))
    pump(len(events))
    for half in range(2):
        for ch in range(NCH):
            rows = pl.ds(half * HALF + ch * CHUNK, CHUNK)
            long, short = ring[half, 6, ch].astype(F32), ring[1 - half, 5, ch].astype(F32)
            gi_out[rows, :] = (part[z, rows].astype(F32) + long + short).astype(BF16)
    swapped(5, y_f.at[o])
    q_out[...] = lax.dot_general(
        inverse, y_f[...].reshape(R, HID), NN, precision=highest, preferred_element_type=F32)
    for cp in sent:
        cp.wait_send()


def local(tokens, w_in, pre_act, grad_hidden, err_state, q_init):
    vm = lambda *shape: pltpu.VMEM(shape, F32)
    vb = lambda *shape: pltpu.VMEM(shape, BF16)
    dma = pltpu.SemaphoreType.DMA
    q_factor, grad_input = pl.pallas_call(
        kernel,
        out_shape=[jax.ShapeDtypeStruct((R, HID), F32), jax.ShapeDtypeStruct((FEAT, TOK), BF16)],
        in_specs=[pl.BlockSpec(memory_space=pl.ANY)] * 6,
        out_specs=[pl.BlockSpec(memory_space=pltpu.VMEM)] * 2,
        scratch_shapes=[vb(TOK, HID), vb(TOK, HID), vm(R, HID), vb(NZ * FEAT, HID), vm(NZ * FEAT, HID),
                        vb(FEAT, TOK), vb(TOK, HID), vb(NZ, FEAT, TOK), vb(2, 7, NCH, CHUNK, TOK)]
        + [vb(NZ, 16, TOK // 2)] * 6
        + [vm(2, NX, 8, FEAT), vm(NX, 8, FEAT), vm(NX, 8, FEAT), vm(NY, 8, FEAT), vm(2, NX, 8, FEAT)]
        + [vm(2, NX, NZ, 8, FEAT), vm(NX, NZ, 8, FEAT), vm(NX, NZ, 8, FEAT), vm(NZ, 8, FEAT), vm(2, NX, NZ, 8, FEAT)]
        + [vm(2, NX, 8, HID), vm(NX, 8, HID), vm(NX, 8, HID), vm(NY, 8, HID), vm(2, NX, 8, HID), vm(R, HID),
           vm(R, 2 * R)]
        + [dma((6, NZ)), dma((6, NZ)), dma((6, NX)), dma((6, NX)), dma((2, NY)), dma((2, NY)), dma((6,)), dma((6,)),
           dma((2, 7, NCH)), dma((2, 7, NCH)), dma((6,))],
        compiler_params=pltpu.CompilerParams(
            collective_id=0, has_side_effects=True, vmem_limit_bytes=56 << 20),
        name="backward",
    )(pre_act, grad_hidden, q_init.T, w_in, err_state[0], tokens.T)
    return (grad_input.T, q_factor.T)


def solution(mesh):
    return jax.shard_map(
        local,
        mesh=mesh,
        in_specs=(
            P("dp", "tensor"),
            P(None, "tensor"),
            P("dp", "tensor"),
            P("dp", "tensor"),
            P("dp", None, "tensor"),
            P("tensor", None),
        ),
        out_specs=(P("dp", "tensor"), P("tensor", None)),
        check_vma=False,
    )
```

```python
import jax
import jax.numpy as jnp
from jax import lax
from jax.experimental import pallas as pl
from jax.experimental.pallas import tpu as pltpu
from jax.sharding import PartitionSpec as P

highest = lax.Precision.HIGHEST
slope_coeff = 0.7978845608
MESH = pl.DeviceIdType.MESH
F32, BF16 = jnp.float32, jnp.bfloat16
NX, NY, NZ = 4, 4, 8
R, TOK, FEAT, HID = 64, 768, 320, 640
NCH = 2
HALF = FEAT // 2
CHUNK = HALF // NCH
HOPS = (4, 3, 3, 2, 2, 1, 1)
NN = (((1,), (0,)), ((), ()))
NT = (((1,), (1,)), ((), ()))


def gelu_slope(argument):
    square = argument * argument
    tangent = jnp.tanh(argument * (slope_coeff + (slope_coeff * 0.044715) * square))
    linear = argument * (slope_coeff + (slope_coeff * 0.134145) * square)
    return 0.5 * (1.0 + tangent) * (1.0 + (1.0 - tangent) * linear)


def halves(value):
    high = value.astype(BF16)
    return high, (value - high.astype(F32)).astype(BF16)


def dot(left, right, dims):
    return lax.dot_general(left, right, dims, preferred_element_type=F32)


def dot_wide(left, right, dims):
    rows = left.shape[0]
    both = dot(jnp.concatenate(halves(left), axis=0), right, dims)
    return both[:rows] + both[rows:]


def dot_both(left, right, dims):
    high, low = halves(right)
    return dot_wide(left, high, dims) + dot(left.astype(BF16), low, dims)


def pair_rows(value):
    n = value.shape[-1] // 2
    return jnp.concatenate([value[..., :n], value[..., n:]], axis=-2)


def unpair_rows(value):
    return jnp.concatenate([value[..., :8, :], value[..., 8:, :]], axis=-1)


def eliminate(work, first, last):
    whole = work[...]
    below = lax.broadcasted_iota(jnp.int32, (R, 1), 0)
    for k in range(first, last):
        row = whole[k:k + 1, :]
        column = whole[:, k:k + 1]
        ratio = jnp.where(below > k, column / whole[k:k + 1, k:k + 1], 0.0)
        whole = whole - ratio * row
    work[...] = whole


def kernel(
    pre_hbm, gh_hbm, qt_hbm, w_hbm, e_hbm, xt_hbm, q_out, gi_out,
    pre, gh, qt, w, e, xt, g, eb, part, ring,
    h_part, h_rs, h_ag, z_part, z_rs, z_ag,
    px_part, px_c, px_x, px_y, pt,
    pe_part, pe_c, pe_x, pe_z, pf,
    y_part, y_c, y_x, y_y, y_f, y_err, work,
    s_z, r_z, s_x, r_x, s_y, r_y, s_c, r_c, s_g, r_g, s_in,
):
    dp, z = lax.axis_index("dp"), lax.axis_index("tensor")
    c, x, y = lax.rem(dp, 2), lax.rem(dp // 2, NX), dp // (2 * NX)
    o = 1 - c

    def at(yy, xx, cc, zz):
        return ((yy * NX + xx) * 2 + cc, zz)

    axes = {
        "z": (NZ, z, lambda j: at(y, x, c, j), s_z, r_z),
        "x": (NX, x, lambda j: at(y, j, c, z), s_x, r_x),
        "y": (NY, y, lambda j: at(j, x, c, z), s_y, r_y),
    }
    sent = []

    def remote(src, dst, ss, rs, dev):
        return pltpu.make_async_remote_copy(
            src_ref=src, dst_ref=dst, send_sem=ss, recv_sem=rs, device_id=dev, device_id_type=MESH)

    def push(src, dst, ss, rs, dev):
        cp = remote(src, dst, ss, rs, dev)
        cp.start()
        sent.append(cp)

    def start(axis, phase, src, dst):
        n, me, dev, ss, rs = axes[axis]
        for k in range(1, n):
            j = lax.rem(me + k, n)
            push(src(j), dst(me), ss.at[phase, k], rs.at[phase, me], dev(j))

    def finish(axis, phase, dst):
        n, me, dev, ss, rs = axes[axis]
        for k in range(1, n):
            j = lax.rem(me + k, n)
            remote(dst(j), dst(j), ss.at[phase, k], rs.at[phase, j], dev(j)).wait_recv()

    def swap(phase, src, dst):
        push(src, dst, s_c.at[phase], r_c.at[phase], at(y, x, o, z))

    def swapped(phase, dst):
        remote(dst, dst, s_c.at[phase], r_c.at[phase], at(y, x, o, z)).wait_recv()

    def shifted(direction, hops):
        return lax.rem(z + (hops if direction == 0 else NZ - hops), NZ)

    def piece(direction, m, ch):
        half = (direction + m) % 2
        return pl.ds(half * HALF + ch * CHUNK, CHUNK)

    def ring_send(direction, m, ch, src):
        push(src, ring.at[direction, m, ch], s_g.at[direction, m, ch], r_g.at[direction, m, ch],
             at(y, x, c, shifted(direction, 1)))

    def ring_first(direction, m):
        for ch in range(NCH):
            ring_send(direction, m, ch, part.at[shifted(direction, HOPS[m]), piece(direction, m, ch)])

    def ring_wait(direction, m, ch):
        slot = ring.at[direction, m, ch]
        remote(slot, slot, s_g.at[direction, m, ch], r_g.at[direction, m, ch],
               at(y, x, c, shifted(direction, 1))).wait_recv()

    def ring_event(m, ch):
        for direction in range(2):
            ring_wait(direction, m, ch)
            if m < 5:
                own = part[shifted(direction, HOPS[m + 2]), piece(direction, m, ch)]
                ring[direction, m, ch] = (ring[direction, m, ch].astype(F32) + own.astype(F32)).astype(BF16)
                ring_send(direction, m + 2, ch, ring.at[direction, m, ch])

    events = [(m, ch) for m in range(7) for ch in range(NCH)]

    def pump(count):
        for _ in range(count):
            if events:
                ring_event(*events.pop(0))

    def product(t):
        rows = w[pl.ds(pl.multiple_of(t * FEAT, FEAT), FEAT), :]
        part[t] = dot(rows, g[...], NT).astype(BF16)

    def drain():
        while sent:
            sent.pop(0).wait_send()

    barrier = pltpu.get_barrier_semaphore()
    for axis in "zyx":
        n, me, dev = axes[axis][:3]
        for k in range(1, n):
            pl.semaphore_signal(barrier, inc=1, device_id=dev(lax.rem(me + k, n)), device_id_type=MESH)
    pl.semaphore_signal(barrier, inc=1, device_id=at(y, x, o, z), device_id_type=MESH)
    loads = [
        pltpu.make_async_copy(src, dst, s_in.at[i])
        for i, (src, dst) in enumerate(
            [(pre_hbm, pre), (gh_hbm, gh), (qt_hbm, qt), (e_hbm, e), (w_hbm, w), (xt_hbm, xt)])
    ]
    for cp in loads:
        cp.start()
    eye = (lax.broadcasted_iota(jnp.int32, (R, R), 0) == lax.broadcasted_iota(jnp.int32, (R, R), 1)).astype(F32)

    loads[0].wait()
    loads[1].wait()

    def activate(i, carry):
        rows = pl.ds(pl.multiple_of(i * 64, 64), 64)
        g[rows, :] = (gh[rows, :].astype(F32) * gelu_slope(pre[rows, :].astype(F32))).astype(BF16)
        return carry

    lax.fori_loop(0, TOK // 64, activate, 0)
    loads[2].wait()
    h_part[...] = pair_rows(dot_wide(qt[...], g[...], NT).reshape(NZ, 8, TOK)).astype(BF16)
    loads[3].wait()

    def error_rows(t, carry):
        rows = pl.ds(pl.multiple_of(t * FEAT, FEAT), FEAT)
        eb[rows, :] = e[rows, :].astype(BF16)
        pe_part[:, :, t] = dot_wide(qt[...], eb[rows, :], NT).reshape(2, NX, 8, FEAT)
        return carry

    lax.fori_loop(0, NZ, error_rows, 0)
    pl.semaphore_wait(barrier, 14)
    start("z", 0, lambda j: h_part.at[j], lambda i: h_rs.at[i])
    swap(0, pe_part.at[o], pe_c)
    h_rs[z] = h_part[z]
    loads[4].wait()
    product(shifted(0, 4))
    ring_first(0, 0)
    ring_first(1, 0)
    product(shifted(0, 3))
    ring_first(0, 1)
    product(shifted(1, 3))
    ring_first(1, 1)
    swapped(0, pe_c)
    pe_c[...] += pe_part[c]
    start("x", 0, lambda j: pe_c.at[j], lambda i: pe_x.at[i])
    pe_x[x] = pe_c[x]
    product(shifted(0, 2))
    finish("z", 0, lambda i: h_rs.at[i])
    h_ag[z] = jnp.sum(h_rs[...].astype(F32), axis=0).astype(BF16)
    start("z", 1, lambda j: h_ag.at[z], lambda i: h_ag.at[i])
    product(shifted(1, 2))
    product(shifted(0, 1))
    product(shifted(1, 1))
    product(z)
    finish("x", 0, lambda i: pe_x.at[i])
    pe_x[x] = pe_x[0] + pe_x[1] + pe_x[2] + pe_x[3]
    start("z", 2, lambda j: pe_x.at[x, j], lambda i: pe_z.at[i])
    pe_z[z] = pe_x[x, z]
    loads[5].wait()
    pump(2)
    finish("z", 1, lambda i: h_ag.at[i])
    h_all = unpair_rows(h_ag[...].astype(F32)).reshape(R, TOK).astype(BF16)
    px_part[...] = dot(h_all, xt[...], NT).reshape(2, NX, 8, FEAT)
    swap(1, px_part.at[o], px_c)
    swapped(1, px_c)
    px_c[...] += px_part[c]
    start("x", 1, lambda j: px_c.at[j], lambda i: px_x.at[i])
    px_x[x] = px_c[x]
    pump(1)
    finish("z", 2, lambda i: pe_z.at[i])
    pe_sum = jnp.sum(pe_z[...], axis=0)
    finish("x", 1, lambda i: px_x.at[i])
    px_y[y] = jnp.sum(px_x[...], axis=0) + pe_sum
    start("y", 0, lambda j: px_y.at[y], lambda i: px_y.at[i])
    pump(1)
    finish("y", 0, lambda i: px_y.at[i])
    p_row = jnp.sum(px_y[...], axis=0)
    pt[c, x] = p_row
    pf[c, x, z] = p_row
    start("x", 2, lambda j: pt.at[c, x], lambda i: pt.at[c, i])
    start("z", 3, lambda j: pf.at[c, x, z], lambda i: pf.at[c, x, i])
    pump(1)
    finish("x", 2, lambda i: pt.at[c, i])
    swap(2, pt.at[c], pt.at[c])
    swapped(2, pt.at[o])
    z_sum = dot_wide(pt[...].reshape(R, FEAT), xt[...], NN).reshape(NZ, 8, TOK)
    z_part[...] = pair_rows(z_sum).astype(BF16)
    start("z", 4, lambda j: z_part.at[j], lambda i: z_rs.at[i])
    z_rs[z] = z_part[z]
    finish("z", 3, lambda i: pf.at[c, x, i])
    start("x", 3, lambda j: pf.at[c, x], lambda i: pf.at[c, i])
    pump(2)
    finish("z", 4, lambda i: z_rs.at[i])
    z_ag[z] = jnp.sum(z_rs[...].astype(F32), axis=0).astype(BF16)
    start("z", 5, lambda j: z_ag.at[z], lambda i: z_ag.at[i])
    finish("x", 3, lambda i: pf.at[c, i])
    swap(3, pf.at[c], pf.at[c])
    pump(1)
    swapped(3, pf.at[o])

    def features(t, gram):
        block = pf[:, :, t].reshape(R, FEAT)
        rows = pl.ds(pl.multiple_of(t * FEAT, FEAT), FEAT)
        y_err[...] += dot_wide(block, eb[rows, :], NN)
        return gram + lax.dot_general(block, block, NT, precision=highest, preferred_element_type=F32)

    y_err[...] = jnp.zeros_like(y_err)
    gram = lax.fori_loop(0, NZ, features, jnp.zeros((R, R), F32))
    work[...] = jnp.concatenate([gram, eye], axis=1)
    pump(1)
    drain()
    finish("z", 5, lambda i: z_ag.at[i])
    z_all = unpair_rows(z_ag[...].astype(F32)).reshape(R, TOK).astype(BF16)
    y_part[...] = (y_err[...] + dot(z_all, g[...], NN)).reshape(2, NX, 8, HID)
    swap(4, y_part.at[o], y_c)
    eliminate(work, 0, 8)
    swapped(4, y_c)
    y_c[...] += y_part[c]
    start("x", 4, lambda j: y_c.at[j], lambda i: y_x.at[i])
    y_x[x] = y_c[x]
    pump(1)
    eliminate(work, 8, 24)
    finish("x", 4, lambda i: y_x.at[i])
    y_y[y] = jnp.sum(y_x[...], axis=0)
    start("y", 1, lambda j: y_y.at[y], lambda i: y_y.at[i])
    pump(1)
    eliminate(work, 24, 40)
    finish("y", 1, lambda i: y_y.at[i])
    y_f[c, x] = jnp.sum(y_y[...], axis=0)
    start("x", 5, lambda j: y_f.at[c, x], lambda i: y_f.at[c, i])
    pump(1)
    eliminate(work, 40, 56)
    finish("x", 5, lambda i: y_f.at[c, i])
    swap(5, y_f.at[c], y_f.at[c])
    eliminate(work, 56, 64)
    diag = jnp.sum(work[:, :R] * eye, axis=1, keepdims=True)
    inverse = work[:, R:] * (lax.rsqrt(diag) * (1.0 / (NX * NY * 2)))
    pump(len(events))
    for half in range(2):
        for ch in range(NCH):
            rows = pl.ds(half * HALF + ch * CHUNK, CHUNK)
            long, short = ring[half, 6, ch].astype(F32), ring[1 - half, 5, ch].astype(F32)
            gi_out[rows, :] = (part[z, rows].astype(F32) + long + short).astype(BF16)
    swapped(5, y_f.at[o])
    q_out[...] = dot_both(inverse, y_f[...].reshape(R, HID), NN)
    drain()


def deliver(q_ref, gi_ref, q_out, gi_out, sems):
    copies = [pltpu.make_async_copy(q_ref, q_out, sems.at[0]), pltpu.make_async_copy(gi_ref, gi_out, sems.at[1])]
    for cp in copies:
        cp.start()
    for cp in copies:
        cp.wait()


def local(tokens, w_in, pre_act, grad_hidden, err_state, q_init):
    vm = lambda *shape: pltpu.VMEM(shape, F32)
    vb = lambda *shape: pltpu.VMEM(shape, BF16)
    dma = pltpu.SemaphoreType.DMA
    q_factor, grad_input = pl.pallas_call(
        kernel,
        out_shape=[jax.ShapeDtypeStruct((R, HID), F32), jax.ShapeDtypeStruct((FEAT, TOK), BF16)],
        in_specs=[pl.BlockSpec(memory_space=pl.ANY)] * 6,
        out_specs=[pl.BlockSpec(memory_space=pltpu.VMEM)] * 2,
        scratch_shapes=[vb(TOK, HID), vb(TOK, HID), vm(R, HID), vb(NZ * FEAT, HID), vm(NZ * FEAT, HID),
                        vb(FEAT, TOK), vb(TOK, HID), vb(NZ * FEAT, HID), vb(NZ, FEAT, TOK), vb(2, 7, NCH, CHUNK, TOK)]
        + [vb(NZ, 16, TOK // 2)] * 6
        + [vm(2, NX, 8, FEAT), vm(NX, 8, FEAT), vm(NX, 8, FEAT), vm(NY, 8, FEAT), vm(2, NX, 8, FEAT)]
        + [vm(2, NX, NZ, 8, FEAT), vm(NX, NZ, 8, FEAT), vm(NX, NZ, 8, FEAT), vm(NZ, 8, FEAT), vm(2, NX, NZ, 8, FEAT)]
        + [vm(2, NX, 8, HID), vm(NX, 8, HID), vm(NX, 8, HID), vm(NY, 8, HID), vm(2, NX, 8, HID), vm(R, HID),
           vm(R, 2 * R)]
        + [dma((6, NZ)), dma((6, NZ)), dma((6, NX)), dma((6, NX)), dma((2, NY)), dma((2, NY)), dma((6,)), dma((6,)),
           dma((2, 7, NCH)), dma((2, 7, NCH)), dma((6,))],
        compiler_params=pltpu.CompilerParams(
            collective_id=0, has_side_effects=True, vmem_limit_bytes=56 << 20),
        name="backward",
    )(pre_act, grad_hidden, q_init.T, w_in, err_state[0], tokens.T)
    q_factor, grad_input = pl.pallas_call(
        deliver,
        out_shape=[jax.ShapeDtypeStruct((R, HID), F32), jax.ShapeDtypeStruct((FEAT, TOK), BF16)],
        in_specs=[pl.BlockSpec(memory_space=pl.ANY)] * 2,
        out_specs=[pl.BlockSpec(memory_space=pl.ANY)] * 2,
        scratch_shapes=[dma((2,))],
        compiler_params=pltpu.CompilerParams(vmem_limit_bytes=56 << 20),
        name="deliver",
    )(q_factor, grad_input)
    return (grad_input.T, q_factor.T)


def solution(mesh):
    return jax.shard_map(
        local,
        mesh=mesh,
        in_specs=(
            P("dp", "tensor"),
            P(None, "tensor"),
            P("dp", "tensor"),
            P("dp", "tensor"),
            P("dp", None, "tensor"),
            P("tensor", None),
        ),
        out_specs=(P("dp", "tensor"), P("tensor", None)),
        check_vma=False,
    )
```

```python
import jax
import jax.numpy as jnp
from jax import lax
from jax.experimental import pallas as pl
from jax.experimental.pallas import tpu as pltpu
from jax.sharding import PartitionSpec as P

highest = lax.Precision.HIGHEST
slope_coeff = 0.7978845608
MESH = pl.DeviceIdType.MESH
F32, BF16 = jnp.float32, jnp.bfloat16
NX, NY, NZ = 4, 4, 8
R, TOK, FEAT, HID = 64, 768, 320, 640
NCH = 2
HALF = FEAT // 2
CHUNK = HALF // NCH
HOPS = (4, 3, 3, 2, 2, 1, 1)
NN = (((1,), (0,)), ((), ()))
NT = (((1,), (1,)), ((), ()))


def gelu_slope(argument):
    square = argument * argument
    tangent = jnp.tanh(argument * (slope_coeff + (slope_coeff * 0.044715) * square))
    linear = argument * (slope_coeff + (slope_coeff * 0.134145) * square)
    return 0.5 * (1.0 + tangent) * (1.0 + (1.0 - tangent) * linear)


def halves(value):
    high = value.astype(BF16)
    return high, (value - high.astype(F32)).astype(BF16)


def dot(left, right, dims):
    return lax.dot_general(left, right, dims, preferred_element_type=F32)


def dot_wide(left, right, dims):
    rows = left.shape[0]
    both = dot(jnp.concatenate(halves(left), axis=0), right, dims)
    return both[:rows] + both[rows:]


def dot_both(left, right, dims):
    high, low = halves(right)
    return dot_wide(left, high, dims) + dot(left.astype(BF16), low, dims)


def pair_rows(value):
    n = value.shape[-1] // 2
    return jnp.concatenate([value[..., :n], value[..., n:]], axis=-2)


def unpair_rows(value):
    return jnp.concatenate([value[..., :8, :], value[..., 8:, :]], axis=-1)


def eliminate(work, first, last, here):
    @pl.when(here)
    def _():
        whole = work[...]
        below = lax.broadcasted_iota(jnp.int32, (R, 1), 0)
        for k in range(first, last):
            row = whole[k:k + 1, :]
            column = whole[:, k:k + 1]
            ratio = jnp.where(below > k, column / whole[k:k + 1, k:k + 1], 0.0)
            whole = whole - ratio * row
        work[...] = whole


def kernel(
    pre_hbm, gh_hbm, qt_hbm, w_hbm, e_hbm, xt_hbm, q_out, gi_out,
    pre, gh, qt, w, e, xt, g, eb, part, ring,
    h_part, h_rs, h_ag, z_part, z_rs, z_ag,
    px_part, px_c, px_x, px_y, pt,
    pe_part, pe_c, pe_x, pe_z, pf,
    y_part, y_c, y_x, y_y, y_f, y_err, work,
    s_z, r_z, s_x, r_x, s_y, r_y, s_c, r_c, s_g, r_g, s_in,
):
    dp, z = lax.axis_index("dp"), lax.axis_index("tensor")
    c, x, y = lax.rem(dp, 2), lax.rem(dp // 2, NX), dp // (2 * NX)
    o = 1 - c

    def at(yy, xx, cc, zz):
        return ((yy * NX + xx) * 2 + cc, zz)

    axes = {
        "z": (NZ, z, lambda j: at(y, x, c, j), s_z, r_z),
        "x": (NX, x, lambda j: at(y, j, c, z), s_x, r_x),
        "y": (NY, y, lambda j: at(j, x, c, z), s_y, r_y),
    }
    sent = []

    def remote(src, dst, ss, rs, dev):
        return pltpu.make_async_remote_copy(
            src_ref=src, dst_ref=dst, send_sem=ss, recv_sem=rs, device_id=dev, device_id_type=MESH)

    def push(src, dst, ss, rs, dev):
        cp = remote(src, dst, ss, rs, dev)
        cp.start()
        sent.append(cp)

    def start(axis, phase, src, dst):
        n, me, dev, ss, rs = axes[axis]
        for k in range(1, n):
            j = lax.rem(me + k, n)
            push(src(j), dst(me), ss.at[phase, k], rs.at[phase, me], dev(j))

    def finish(axis, phase, dst):
        n, me, dev, ss, rs = axes[axis]
        for k in range(1, n):
            j = lax.rem(me + k, n)
            remote(dst(j), dst(j), ss.at[phase, k], rs.at[phase, j], dev(j)).wait_recv()

    def swap(phase, src, dst):
        push(src, dst, s_c.at[phase], r_c.at[phase], at(y, x, o, z))

    def swapped(phase, dst):
        remote(dst, dst, s_c.at[phase], r_c.at[phase], at(y, x, o, z)).wait_recv()

    def shifted(direction, hops):
        return lax.rem(z + (hops if direction == 0 else NZ - hops), NZ)

    def piece(direction, m, ch):
        half = (direction + m) % 2
        return pl.ds(half * HALF + ch * CHUNK, CHUNK)

    def ring_send(direction, m, ch, src):
        push(src, ring.at[direction, m, ch], s_g.at[direction, m, ch], r_g.at[direction, m, ch],
             at(y, x, c, shifted(direction, 1)))

    def ring_first(direction, m):
        for ch in range(NCH):
            ring_send(direction, m, ch, part.at[shifted(direction, HOPS[m]), piece(direction, m, ch)])

    def ring_wait(direction, m, ch):
        slot = ring.at[direction, m, ch]
        remote(slot, slot, s_g.at[direction, m, ch], r_g.at[direction, m, ch],
               at(y, x, c, shifted(direction, 1))).wait_recv()

    def ring_event(m, ch):
        for direction in range(2):
            ring_wait(direction, m, ch)
            if m < 5:
                own = part[shifted(direction, HOPS[m + 2]), piece(direction, m, ch)]
                ring[direction, m, ch] = (ring[direction, m, ch].astype(F32) + own.astype(F32)).astype(BF16)
                ring_send(direction, m + 2, ch, ring.at[direction, m, ch])

    events = [(m, ch) for m in range(7) for ch in range(NCH)]

    def pump(count):
        for _ in range(count):
            if events:
                ring_event(*events.pop(0))

    def product(t):
        rows = w[pl.ds(pl.multiple_of(t * FEAT, FEAT), FEAT), :]
        part[t] = dot(rows, g[...], NT).astype(BF16)

    def drain():
        while sent:
            sent.pop(0).wait_send()

    def load(src, dst, i):
        cp = pltpu.make_async_copy(src, dst, s_in.at[i])
        cp.start()
        return cp

    def block(t):
        return pl.ds(pl.multiple_of(t * FEAT, FEAT), FEAT)

    order = [shifted(0, 4), shifted(0, 3), shifted(1, 3), shifted(0, 2), shifted(1, 2), shifted(0, 1), shifted(1, 1), z]

    def load_w(i):
        return load(w_hbm.at[block(order[i])], w.at[block(order[i])], 4 + i)

    def load_e(t):
        return pltpu.make_async_copy(e_hbm.at[block(t)], e.at[block(t)], s_in.at[12 + t])

    loads = [load(pre_hbm, pre, 0), load(gh_hbm, gh, 1), load(qt_hbm, qt, 2)]
    barrier = pltpu.get_barrier_semaphore()
    for axis in "zyx":
        n, me, dev = axes[axis][:3]
        for k in range(1, n):
            pl.semaphore_signal(barrier, inc=1, device_id=dev(lax.rem(me + k, n)), device_id_type=MESH)
    pl.semaphore_signal(barrier, inc=1, device_id=at(y, x, o, z), device_id_type=MESH)
    eye = (lax.broadcasted_iota(jnp.int32, (R, R), 0) == lax.broadcasted_iota(jnp.int32, (R, R), 1)).astype(F32)

    loads[0].wait()
    loads[1].wait()
    w_loads = [load_w(i) for i in range(3)]
    for t in range(NZ):
        load_e(t).start()
    w_loads += [load_w(i) for i in range(3, NZ)]
    x_load = load(xt_hbm, xt, 3)

    def activate(i, carry):
        rows = pl.ds(pl.multiple_of(i * 32, 32), 32)
        g[rows, :] = (gh[rows, :].astype(F32) * gelu_slope(pre[rows, :].astype(F32))).astype(BF16)
        return carry

    lax.fori_loop(0, TOK // 32, activate, 0)
    loads[2].wait()
    h_part[...] = pair_rows(dot_wide(qt[...], g[...], NT).reshape(NZ, 8, TOK)).astype(BF16)
    pl.semaphore_wait(barrier, 14)
    start("z", 0, lambda j: h_part.at[j], lambda i: h_rs.at[i])
    h_rs[z] = h_part[z]
    w_loads[0].wait()
    product(order[0])
    ring_first(0, 0)
    ring_first(1, 0)

    def error_rows(t, carry):
        load_e(t).wait()
        eb[block(t), :] = e[block(t), :].astype(BF16)
        pe_part[:, :, t] = dot_wide(qt[...], eb[block(t), :], NT).reshape(2, NX, 8, FEAT)
        return carry

    lax.fori_loop(0, NZ, error_rows, 0)
    swap(0, pe_part.at[o], pe_c)
    w_loads[1].wait()
    product(order[1])
    ring_first(0, 1)
    w_loads[2].wait()
    product(order[2])
    ring_first(1, 1)
    swapped(0, pe_c)
    pe_c[...] += pe_part[c]
    start("x", 0, lambda j: pe_c.at[j], lambda i: pe_x.at[i])
    pe_x[x] = pe_c[x]
    finish("z", 0, lambda i: h_rs.at[i])
    h_ag[z] = jnp.sum(h_rs[...].astype(F32), axis=0).astype(BF16)
    start("z", 1, lambda j: h_ag.at[z], lambda i: h_ag.at[i])
    for cp in w_loads[3:]:
        cp.wait()

    def products(k, carry):
        product(lax.rem(z + NZ - 2 + k, NZ))
        return carry

    lax.fori_loop(0, 5, products, 0)
    finish("x", 0, lambda i: pe_x.at[i])
    pe_x[x] = pe_x[0] + pe_x[1] + pe_x[2] + pe_x[3]
    start("z", 2, lambda j: pe_x.at[x, j], lambda i: pe_z.at[i])
    pe_z[z] = pe_x[x, z]
    x_load.wait()
    pump(1)
    finish("z", 1, lambda i: h_ag.at[i])
    h_all = unpair_rows(h_ag[...].astype(F32)).reshape(R, TOK).astype(BF16)
    px_part[...] = dot(h_all, xt[...], NT).reshape(2, NX, 8, FEAT)
    swap(1, px_part.at[o], px_c)
    swapped(1, px_c)
    px_c[...] += px_part[c]
    start("x", 1, lambda j: px_c.at[j], lambda i: px_x.at[i])
    px_x[x] = px_c[x]
    pump(2)
    finish("z", 2, lambda i: pe_z.at[i])
    pe_sum = jnp.sum(pe_z[...], axis=0)
    finish("x", 1, lambda i: px_x.at[i])
    px_y[y] = jnp.sum(px_x[...], axis=0) + pe_sum
    start("y", 0, lambda j: px_y.at[y], lambda i: px_y.at[i])
    pump(1)
    finish("y", 0, lambda i: px_y.at[i])
    p_row = jnp.sum(px_y[...], axis=0)
    pt[c, x] = p_row
    pf[c, x, z] = p_row
    start("x", 2, lambda j: pt.at[c, x], lambda i: pt.at[c, i])
    start("z", 3, lambda j: pf.at[c, x, z], lambda i: pf.at[c, x, i])
    pump(1)
    finish("x", 2, lambda i: pt.at[c, i])
    swap(2, pt.at[c], pt.at[c])
    swapped(2, pt.at[o])
    z_sum = dot_wide(pt[...].reshape(R, FEAT), xt[...], NN).reshape(NZ, 8, TOK)
    z_part[...] = pair_rows(z_sum).astype(BF16)
    start("z", 4, lambda j: z_part.at[j], lambda i: z_rs.at[i])
    z_rs[z] = z_part[z]
    finish("z", 3, lambda i: pf.at[c, x, i])
    start("x", 3, lambda j: pf.at[c, x], lambda i: pf.at[c, i])
    pump(2)
    finish("z", 4, lambda i: z_rs.at[i])
    z_ag[z] = jnp.sum(z_rs[...].astype(F32), axis=0).astype(BF16)
    start("z", 5, lambda j: z_ag.at[z], lambda i: z_ag.at[i])
    finish("x", 3, lambda i: pf.at[c, i])
    swap(3, pf.at[c], pf.at[c])
    pump(1)
    swapped(3, pf.at[o])

    def features(t, gram):
        rows = pf[:, :, t].reshape(R, FEAT)
        y_err[...] += dot_wide(rows, eb[block(t), :], NN)
        return gram + lax.dot_general(rows, rows, NT, precision=highest, preferred_element_type=F32)

    y_err[...] = jnp.zeros_like(y_err)
    gram = lax.fori_loop(0, NZ, features, jnp.zeros((R, R), F32))
    work[...] = jnp.concatenate([gram, eye], axis=1)
    pump(1)
    drain()
    finish("z", 5, lambda i: z_ag.at[i])
    z_all = unpair_rows(z_ag[...].astype(F32)).reshape(R, TOK).astype(BF16)
    y_part[...] = (y_err[...] + dot(z_all, g[...], NN)).reshape(2, NX, 8, HID)
    swap(4, y_part.at[o], y_c)
    eliminate(work, 0, 8, z >= 0)
    swapped(4, y_c)
    y_c[...] += y_part[c]
    start("x", 4, lambda j: y_c.at[j], lambda i: y_x.at[i])
    y_x[x] = y_c[x]
    pump(1)
    eliminate(work, 8, 24, z >= 0)
    finish("x", 4, lambda i: y_x.at[i])
    y_y[y] = jnp.sum(y_x[...], axis=0)
    start("y", 1, lambda j: y_y.at[y], lambda i: y_y.at[i])
    pump(1)
    eliminate(work, 24, 40, z >= 0)
    finish("y", 1, lambda i: y_y.at[i])
    y_f[c, x] = jnp.sum(y_y[...], axis=0)
    start("x", 5, lambda j: y_f.at[c, x], lambda i: y_f.at[c, i])
    pump(1)
    eliminate(work, 40, 56, z >= 0)
    finish("x", 5, lambda i: y_f.at[c, i])
    swap(5, y_f.at[c], y_f.at[c])
    eliminate(work, 56, 64, z >= 0)
    diag = jnp.sum(work[:, :R] * eye, axis=1, keepdims=True)
    inverse = work[:, R:] * (lax.rsqrt(diag) * (1.0 / (NX * NY * 2)))
    pump(len(events))
    for half in range(2):
        for ch in range(NCH):
            rows = pl.ds(half * HALF + ch * CHUNK, CHUNK)
            long, short = ring[half, 6, ch].astype(F32), ring[1 - half, 5, ch].astype(F32)
            gi_out[rows, :] = (part[z, rows].astype(F32) + long + short).astype(BF16)
    swapped(5, y_f.at[o])
    q_out[...] = dot_both(inverse, y_f[...].reshape(R, HID), NN)
    drain()


def deliver(q_ref, gi_ref, q_out, gi_out):
    q_out[...] = q_ref[...]
    gi_out[...] = gi_ref[...]


def local(tokens, w_in, pre_act, grad_hidden, err_state, q_init):
    vm = lambda *shape: pltpu.VMEM(shape, F32)
    vb = lambda *shape: pltpu.VMEM(shape, BF16)
    dma = pltpu.SemaphoreType.DMA
    q_factor, grad_input = pl.pallas_call(
        kernel,
        out_shape=[jax.ShapeDtypeStruct((R, HID), F32), jax.ShapeDtypeStruct((FEAT, TOK), BF16)],
        in_specs=[pl.BlockSpec(memory_space=pl.ANY)] * 6,
        out_specs=[pl.BlockSpec(memory_space=pltpu.VMEM)] * 2,
        scratch_shapes=[vb(TOK, HID), vb(TOK, HID), vm(R, HID), vb(NZ * FEAT, HID), vm(NZ * FEAT, HID),
                        vb(FEAT, TOK), vb(TOK, HID), vb(NZ * FEAT, HID), vb(NZ, FEAT, TOK), vb(2, 7, NCH, CHUNK, TOK)]
        + [vb(NZ, 16, TOK // 2)] * 6
        + [vm(2, NX, 8, FEAT), vm(NX, 8, FEAT), vm(NX, 8, FEAT), vm(NY, 8, FEAT), vm(2, NX, 8, FEAT)]
        + [vm(2, NX, NZ, 8, FEAT), vm(NX, NZ, 8, FEAT), vm(NX, NZ, 8, FEAT), vm(NZ, 8, FEAT), vm(2, NX, NZ, 8, FEAT)]
        + [vm(2, NX, 8, HID), vm(NX, 8, HID), vm(NX, 8, HID), vm(NY, 8, HID), vm(2, NX, 8, HID), vm(R, HID),
           vm(R, 2 * R)]
        + [dma((6, NZ)), dma((6, NZ)), dma((6, NX)), dma((6, NX)), dma((2, NY)), dma((2, NY)), dma((6,)), dma((6,)),
           dma((2, 7, NCH)), dma((2, 7, NCH)), dma((20,))],
        compiler_params=pltpu.CompilerParams(
            collective_id=0, has_side_effects=True, vmem_limit_bytes=56 << 20),
        name="backward",
    )(pre_act, grad_hidden, q_init.T, w_in, err_state[0], tokens.T)
    q_factor, grad_input = pl.pallas_call(
        deliver,
        out_shape=[jax.ShapeDtypeStruct((R, HID), F32), jax.ShapeDtypeStruct((FEAT, TOK), BF16)],
        in_specs=[pl.BlockSpec(memory_space=pltpu.VMEM)] * 2,
        out_specs=[pl.BlockSpec(memory_space=pltpu.VMEM)] * 2,
        compiler_params=pltpu.CompilerParams(vmem_limit_bytes=56 << 20),
        name="deliver",
    )(q_factor, grad_input)
    return (grad_input.T, q_factor.T)


def solution(mesh):
    return jax.shard_map(
        local,
        mesh=mesh,
        in_specs=(
            P("dp", "tensor"),
            P(None, "tensor"),
            P("dp", "tensor"),
            P("dp", "tensor"),
            P("dp", None, "tensor"),
            P("tensor", None),
        ),
        out_specs=(P("dp", "tensor"), P("tensor", None)),
        check_vma=False,
    )
```

```python
import jax
import jax.numpy as jnp
from jax import lax
from jax.experimental import pallas as pl
from jax.experimental.pallas import tpu as pltpu
from jax.sharding import PartitionSpec as P

highest = lax.Precision.HIGHEST
slope_coeff = 0.7978845608
MESH = pl.DeviceIdType.MESH
F32, BF16 = jnp.float32, jnp.bfloat16
NX, NY, NZ = 4, 4, 8
R, TOK, FEAT, HID = 64, 768, 320, 640
NCH = 2
HALF = FEAT // 2
CHUNK = HALF // NCH
HOPS = (4, 3, 3, 2, 2, 1, 1)
SENDS = dict(a=2, b=0, c=0, d=1, e=1, f=1, g=1, h=1, i=1, j=0, k=2, l=0, m=1, n=1, o=1, p=1, q=0)
NN = (((1,), (0,)), ((), ()))
NT = (((1,), (1,)), ((), ()))


def gelu_slope(argument):
    square = argument * argument
    tangent = jnp.tanh(argument * (slope_coeff + (slope_coeff * 0.044715) * square))
    linear = argument * (slope_coeff + (slope_coeff * 0.134145) * square)
    return 0.5 * (1.0 + tangent) * (1.0 + (1.0 - tangent) * linear)


def halves(value):
    high = value.astype(BF16)
    return high, (value - high.astype(F32)).astype(BF16)


def dot(left, right, dims):
    return lax.dot_general(left, right, dims, preferred_element_type=F32)


def dot_wide(left, right, dims):
    rows = left.shape[0]
    both = dot(jnp.concatenate(halves(left), axis=0), right, dims)
    return both[:rows] + both[rows:]


def dot_both(left, right, dims):
    high, low = halves(right)
    return dot_wide(left, high, dims) + dot(left.astype(BF16), low, dims)


def pair_rows(value):
    n = value.shape[-1] // 2
    return jnp.concatenate([value[..., :n], value[..., n:]], axis=-2)


def unpair_rows(value):
    return jnp.concatenate([value[..., :8, :], value[..., 8:, :]], axis=-1)


def eliminate(work, first, last, here):
    @pl.when(here)
    def _():
        whole = work[...]
        below = lax.broadcasted_iota(jnp.int32, (R, 1), 0)
        for k in range(first, last):
            row = whole[k:k + 1, :]
            column = whole[:, k:k + 1]
            ratio = jnp.where(below > k, column / whole[k:k + 1, k:k + 1], 0.0)
            whole = whole - ratio * row
        work[...] = whole


def kernel(
    pre_hbm, gh_hbm, qt_hbm, w_hbm, e_hbm, xt_hbm, q_out, gi_out,
    pre, gh, qt, w, e, xt, g, eb, part, ring,
    h_part, h_rs, h_ag, z_part, z_rs, z_ag,
    px_part, px_c, px_x, px_y, pt,
    pe_part, pe_c, pe_x, pe_z, pf,
    y_part, y_c, y_x, y_y, y_f, y_err, work,
    s_z, r_z, s_x, r_x, s_y, r_y, s_c, r_c, s_g, r_g, s_in,
):
    dp, z = lax.axis_index("dp"), lax.axis_index("tensor")
    c, x, y = lax.rem(dp, 2), lax.rem(dp // 2, NX), dp // (2 * NX)
    o = 1 - c

    def at(yy, xx, cc, zz):
        return ((yy * NX + xx) * 2 + cc, zz)

    axes = {
        "z": (NZ, z, lambda j: at(y, x, c, j), s_z, r_z),
        "x": (NX, x, lambda j: at(y, j, c, z), s_x, r_x),
        "y": (NY, y, lambda j: at(j, x, c, z), s_y, r_y),
    }
    sent = []

    def remote(src, dst, ss, rs, dev):
        return pltpu.make_async_remote_copy(
            src_ref=src, dst_ref=dst, send_sem=ss, recv_sem=rs, device_id=dev, device_id_type=MESH)

    def push(src, dst, ss, rs, dev):
        cp = remote(src, dst, ss, rs, dev)
        cp.start()
        sent.append(cp)

    def start(axis, phase, src, dst):
        n, me, dev, ss, rs = axes[axis]
        for k in range(1, n):
            j = lax.rem(me + k, n)
            push(src(j), dst(me), ss.at[phase, k], rs.at[phase, me], dev(j))

    def finish(axis, phase, dst):
        n, me, dev, ss, rs = axes[axis]
        for k in range(1, n):
            j = lax.rem(me + k, n)
            remote(dst(j), dst(j), ss.at[phase, k], rs.at[phase, j], dev(j)).wait_recv()

    def swap(phase, src, dst):
        push(src, dst, s_c.at[phase], r_c.at[phase], at(y, x, o, z))

    def swapped(phase, dst):
        remote(dst, dst, s_c.at[phase], r_c.at[phase], at(y, x, o, z)).wait_recv()

    def shifted(direction, hops):
        return lax.rem(z + (hops if direction == 0 else NZ - hops), NZ)

    def piece(direction, m, ch):
        half = (direction + m) % 2
        return pl.ds(half * HALF + ch * CHUNK, CHUNK)

    def ring_send(direction, m, ch, src):
        push(src, ring.at[direction, m, ch], s_g.at[direction, m, ch], r_g.at[direction, m, ch],
             at(y, x, c, shifted(direction, 1)))

    def ring_wait(direction, m, ch):
        slot = ring.at[direction, m, ch]
        remote(slot, slot, s_g.at[direction, m, ch], r_g.at[direction, m, ch],
               at(y, x, c, shifted(direction, 1))).wait_recv()

    todo = [(m, ch) for m in range(7) for ch in range(NCH)]

    def advance(count):
        for m, ch in todo[:count]:
            for direction in range(2):
                mine = part.at[shifted(direction, HOPS[m]), piece(direction, m, ch)]
                if m < 2:
                    ring_send(direction, m, ch, mine)
                else:
                    ring_wait(direction, m - 2, ch)
                    slot = ring.at[direction, m - 2, ch]
                    slot[...] = (slot[...].astype(F32) + mine[...].astype(F32)).astype(BF16)
                    ring_send(direction, m, ch, slot)
        del todo[:count]

    def product(t):
        rows = w[pl.ds(pl.multiple_of(t * FEAT, FEAT), FEAT), :]
        part[t] = dot(rows, g[...], NT).astype(BF16)

    def drain():
        while sent:
            sent.pop(0).wait_send()

    def load(src, dst, i):
        cp = pltpu.make_async_copy(src, dst, s_in.at[i])
        cp.start()
        return cp

    def block(t):
        return pl.ds(pl.multiple_of(t * FEAT, FEAT), FEAT)

    order = [shifted(0, 4), shifted(0, 3), shifted(1, 3), shifted(0, 2), shifted(1, 2), shifted(0, 1), shifted(1, 1), z]

    def load_w(i):
        return load(w_hbm.at[block(order[i])], w.at[block(order[i])], 4 + i)

    def load_e(t):
        return pltpu.make_async_copy(e_hbm.at[block(t)], e.at[block(t)], s_in.at[12 + t])

    loads = [load(pre_hbm, pre, 0), load(gh_hbm, gh, 1), load(qt_hbm, qt, 2)]
    barrier = pltpu.get_barrier_semaphore()
    for axis in "zyx":
        n, me, dev = axes[axis][:3]
        for k in range(1, n):
            pl.semaphore_signal(barrier, inc=1, device_id=dev(lax.rem(me + k, n)), device_id_type=MESH)
    pl.semaphore_signal(barrier, inc=1, device_id=at(y, x, o, z), device_id_type=MESH)
    eye = (lax.broadcasted_iota(jnp.int32, (R, R), 0) == lax.broadcasted_iota(jnp.int32, (R, R), 1)).astype(F32)

    loads[0].wait()
    loads[1].wait()
    w_loads = [load_w(i) for i in range(3)]
    for t in range(NZ):
        load_e(t).start()
    w_loads += [load_w(i) for i in range(3, NZ)]
    x_load = load(xt_hbm, xt, 3)

    def activate(i, carry):
        rows = pl.ds(pl.multiple_of(i * 32, 32), 32)
        g[rows, :] = (gh[rows, :].astype(F32) * gelu_slope(pre[rows, :].astype(F32))).astype(BF16)
        return carry

    lax.fori_loop(0, TOK // 32, activate, 0)
    loads[2].wait()
    h_part[...] = pair_rows(dot_wide(qt[...], g[...], NT).reshape(NZ, 8, TOK)).astype(BF16)
    pl.semaphore_wait(barrier, 14)
    start("z", 0, lambda j: h_part.at[j], lambda i: h_rs.at[i])
    h_rs[z] = h_part[z]
    w_loads[0].wait()
    product(order[0])
    advance(SENDS["a"])

    def error_rows(t, carry):
        load_e(t).wait()
        eb[block(t), :] = e[block(t), :].astype(BF16)
        pe_part[:, :, t] = dot_wide(qt[...], eb[block(t), :], NT).reshape(2, NX, 8, FEAT)
        return carry

    lax.fori_loop(0, NZ, error_rows, 0)
    swap(0, pe_part.at[o], pe_c)
    w_loads[1].wait()
    product(order[1])
    w_loads[2].wait()
    product(order[2])
    advance(SENDS["b"])
    swapped(0, pe_c)
    pe_c[...] += pe_part[c]
    start("x", 0, lambda j: pe_c.at[j], lambda i: pe_x.at[i])
    pe_x[x] = pe_c[x]
    finish("z", 0, lambda i: h_rs.at[i])
    h_ag[z] = jnp.sum(h_rs[...].astype(F32), axis=0).astype(BF16)
    start("z", 1, lambda j: h_ag.at[z], lambda i: h_ag.at[i])
    advance(SENDS["c"])
    for cp in w_loads[3:]:
        cp.wait()

    def products(k, carry):
        product(lax.rem(z + NZ - 2 + k, NZ))
        return carry

    lax.fori_loop(0, 5, products, 0)
    finish("x", 0, lambda i: pe_x.at[i])
    pe_x[x] = pe_x[0] + pe_x[1] + pe_x[2] + pe_x[3]
    start("z", 2, lambda j: pe_x.at[x, j], lambda i: pe_z.at[i])
    pe_z[z] = pe_x[x, z]
    x_load.wait()
    advance(SENDS["d"])
    finish("z", 1, lambda i: h_ag.at[i])
    h_all = unpair_rows(h_ag[...].astype(F32)).reshape(R, TOK).astype(BF16)
    px_part[...] = dot(h_all, xt[...], NT).reshape(2, NX, 8, FEAT)
    swap(1, px_part.at[o], px_c)
    advance(SENDS["e"])
    swapped(1, px_c)
    px_c[...] += px_part[c]
    start("x", 1, lambda j: px_c.at[j], lambda i: px_x.at[i])
    px_x[x] = px_c[x]
    advance(SENDS["f"])
    finish("z", 2, lambda i: pe_z.at[i])
    pe_sum = jnp.sum(pe_z[...], axis=0)
    finish("x", 1, lambda i: px_x.at[i])
    px_y[y] = jnp.sum(px_x[...], axis=0) + pe_sum
    start("y", 0, lambda j: px_y.at[y], lambda i: px_y.at[i])
    advance(SENDS["g"])
    finish("y", 0, lambda i: px_y.at[i])
    p_row = jnp.sum(px_y[...], axis=0)
    pt[c, x] = p_row
    pf[c, x, z] = p_row
    start("x", 2, lambda j: pt.at[c, x], lambda i: pt.at[c, i])
    start("z", 3, lambda j: pf.at[c, x, z], lambda i: pf.at[c, x, i])
    advance(SENDS["h"])
    finish("x", 2, lambda i: pt.at[c, i])
    swap(2, pt.at[c], pt.at[c])
    swapped(2, pt.at[o])
    z_sum = dot_wide(pt[...].reshape(R, FEAT), xt[...], NN).reshape(NZ, 8, TOK)
    z_part[...] = pair_rows(z_sum).astype(BF16)
    start("z", 4, lambda j: z_part.at[j], lambda i: z_rs.at[i])
    z_rs[z] = z_part[z]
    advance(SENDS["i"])
    finish("z", 3, lambda i: pf.at[c, x, i])
    start("x", 3, lambda j: pf.at[c, x], lambda i: pf.at[c, i])
    advance(SENDS["j"])
    finish("z", 4, lambda i: z_rs.at[i])
    z_ag[z] = jnp.sum(z_rs[...].astype(F32), axis=0).astype(BF16)
    start("z", 5, lambda j: z_ag.at[z], lambda i: z_ag.at[i])
    advance(SENDS["k"])
    finish("x", 3, lambda i: pf.at[c, i])
    swap(3, pf.at[c], pf.at[c])
    swapped(3, pf.at[o])

    def features(t, gram):
        rows = pf[:, :, t].reshape(R, FEAT)
        y_err[...] += dot_wide(rows, eb[block(t), :], NN)
        return gram + lax.dot_general(rows, rows, NT, precision=highest, preferred_element_type=F32)

    y_err[...] = jnp.zeros_like(y_err)
    gram = lax.fori_loop(0, NZ, features, jnp.zeros((R, R), F32))
    work[...] = jnp.concatenate([gram, eye], axis=1)
    advance(SENDS["l"])
    drain()
    finish("z", 5, lambda i: z_ag.at[i])
    z_all = unpair_rows(z_ag[...].astype(F32)).reshape(R, TOK).astype(BF16)
    y_part[...] = (y_err[...] + dot(z_all, g[...], NN)).reshape(2, NX, 8, HID)
    swap(4, y_part.at[o], y_c)
    advance(SENDS["m"])
    eliminate(work, 0, 8, z >= 0)
    swapped(4, y_c)
    y_c[...] += y_part[c]
    start("x", 4, lambda j: y_c.at[j], lambda i: y_x.at[i])
    y_x[x] = y_c[x]
    advance(SENDS["n"])
    eliminate(work, 8, 24, z >= 0)
    finish("x", 4, lambda i: y_x.at[i])
    y_y[y] = jnp.sum(y_x[...], axis=0)
    start("y", 1, lambda j: y_y.at[y], lambda i: y_y.at[i])
    advance(SENDS["o"])
    eliminate(work, 24, 40, z >= 0)
    finish("y", 1, lambda i: y_y.at[i])
    y_f[c, x] = jnp.sum(y_y[...], axis=0)
    start("x", 5, lambda j: y_f.at[c, x], lambda i: y_f.at[c, i])
    advance(SENDS["p"])
    eliminate(work, 40, 56, z >= 0)
    finish("x", 5, lambda i: y_f.at[c, i])
    swap(5, y_f.at[c], y_f.at[c])
    advance(SENDS["q"])
    eliminate(work, 56, 64, z >= 0)
    diag = jnp.sum(work[:, :R] * eye, axis=1, keepdims=True)
    inverse = work[:, R:] * (lax.rsqrt(diag) * (1.0 / (NX * NY * 2)))
    advance(len(todo))
    for m in (5, 6):
        for ch in range(NCH):
            for direction in range(2):
                ring_wait(direction, m, ch)
    for half in range(2):
        for ch in range(NCH):
            rows = pl.ds(half * HALF + ch * CHUNK, CHUNK)
            long, short = ring[half, 6, ch].astype(F32), ring[1 - half, 5, ch].astype(F32)
            gi_out[rows, :] = (part[z, rows].astype(F32) + long + short).astype(BF16)
    swapped(5, y_f.at[o])
    q_out[...] = dot_both(inverse, y_f[...].reshape(R, HID), NN)
    drain()


def deliver(q_ref, gi_ref, q_out, gi_out):
    q_out[...] = q_ref[...]
    gi_out[...] = gi_ref[...]


def local(tokens, w_in, pre_act, grad_hidden, err_state, q_init):
    vm = lambda *shape: pltpu.VMEM(shape, F32)
    vb = lambda *shape: pltpu.VMEM(shape, BF16)
    dma = pltpu.SemaphoreType.DMA
    q_factor, grad_input = pl.pallas_call(
        kernel,
        out_shape=[jax.ShapeDtypeStruct((R, HID), F32), jax.ShapeDtypeStruct((FEAT, TOK), BF16)],
        in_specs=[pl.BlockSpec(memory_space=pl.ANY)] * 6,
        out_specs=[pl.BlockSpec(memory_space=pltpu.VMEM)] * 2,
        scratch_shapes=[vb(TOK, HID), vb(TOK, HID), vm(R, HID), vb(NZ * FEAT, HID), vm(NZ * FEAT, HID),
                        vb(FEAT, TOK), vb(TOK, HID), vb(NZ * FEAT, HID), vb(NZ, FEAT, TOK), vb(2, 7, NCH, CHUNK, TOK)]
        + [vb(NZ, 16, TOK // 2)] * 6
        + [vm(2, NX, 8, FEAT), vm(NX, 8, FEAT), vm(NX, 8, FEAT), vm(NY, 8, FEAT), vm(2, NX, 8, FEAT)]
        + [vm(2, NX, NZ, 8, FEAT), vm(NX, NZ, 8, FEAT), vm(NX, NZ, 8, FEAT), vm(NZ, 8, FEAT), vm(2, NX, NZ, 8, FEAT)]
        + [vm(2, NX, 8, HID), vm(NX, 8, HID), vm(NX, 8, HID), vm(NY, 8, HID), vm(2, NX, 8, HID), vm(R, HID),
           vm(R, 2 * R)]
        + [dma((6, NZ)), dma((6, NZ)), dma((6, NX)), dma((6, NX)), dma((2, NY)), dma((2, NY)), dma((6,)), dma((6,)),
           dma((2, 7, NCH)), dma((2, 7, NCH)), dma((20,))],
        compiler_params=pltpu.CompilerParams(
            collective_id=0, has_side_effects=True, vmem_limit_bytes=56 << 20),
        name="backward",
    )(pre_act, grad_hidden, q_init.T, w_in, err_state[0], tokens.T)
    q_factor, grad_input = pl.pallas_call(
        deliver,
        out_shape=[jax.ShapeDtypeStruct((R, HID), F32), jax.ShapeDtypeStruct((FEAT, TOK), BF16)],
        in_specs=[pl.BlockSpec(memory_space=pltpu.VMEM)] * 2,
        out_specs=[pl.BlockSpec(memory_space=pltpu.VMEM)] * 2,
        compiler_params=pltpu.CompilerParams(vmem_limit_bytes=56 << 20),
        name="deliver",
    )(q_factor, grad_input)
    return (grad_input.T, q_factor.T)


def solution(mesh):
    return jax.shard_map(
        local,
        mesh=mesh,
        in_specs=(
            P("dp", "tensor"),
            P(None, "tensor"),
            P("dp", "tensor"),
            P("dp", "tensor"),
            P("dp", None, "tensor"),
            P("tensor", None),
        ),
        out_specs=(P("dp", "tensor"), P("tensor", None)),
        check_vma=False,
    )
```

```python
import jax
import jax.numpy as jnp
from jax import lax
from jax.experimental import pallas as pl
from jax.experimental.pallas import tpu as pltpu
from jax.sharding import PartitionSpec as P

slope_coeff = 0.7978845608
MESH = pl.DeviceIdType.MESH
F32, BF16 = jnp.float32, jnp.bfloat16
NX, NY, NZ = 4, 4, 8
R, TOK, FEAT, HID = 64, 768, 320, 640
NCH = 2
HALF = FEAT // 2
CHUNK = HALF // NCH
HOPS = (4, 3, 3, 2, 2, 1, 1)
SENDS = dict(a=2, b=0, c=0, d=1, e=1, f=1, g=1, h=1, i=1, j=0, k=1, l=0, m=2, n=1, o=1, p=1, q=0)
FAR = {4: (2, 1, 3), 8: (4, 3, 5, 2, 6, 1, 7)}
NN = (((1,), (0,)), ((), ()))
NT = (((1,), (1,)), ((), ()))


def gelu_slope(argument):
    square = argument * argument
    tangent = jnp.tanh(argument * (slope_coeff + (slope_coeff * 0.044715) * square))
    linear = argument * (slope_coeff + (slope_coeff * 0.134145) * square)
    return 0.5 * (1.0 + tangent) * (1.0 + (1.0 - tangent) * linear)


def halves(value):
    high = value.astype(BF16)
    return high, (value - high.astype(F32)).astype(BF16)


def dot(left, right, dims):
    return lax.dot_general(left, right, dims, preferred_element_type=F32)


def dot_wide(left, right, dims):
    rows = left.shape[0]
    both = dot(jnp.concatenate(halves(left), axis=0), right, dims)
    return both[:rows] + both[rows:]


def dot_both(left, right, dims):
    high, low = halves(right)
    return dot_wide(left, high, dims) + dot(left.astype(BF16), low, dims)


def pair_rows(value):
    n = value.shape[-1] // 2
    return jnp.concatenate([value[..., :n], value[..., n:]], axis=-2)


def unpair_rows(value):
    return jnp.concatenate([value[..., :8, :], value[..., 8:, :]], axis=-1)


def eliminate(work, first, last, here):
    @pl.when(here)
    def _():
        whole = work[...]
        below = lax.broadcasted_iota(jnp.int32, (R, 1), 0)
        for k in range(first, last):
            row = whole[k:k + 1, :]
            column = whole[:, k:k + 1]
            ratio = jnp.where(below > k, column / whole[k:k + 1, k:k + 1], 0.0)
            whole = whole - ratio * row
        work[...] = whole


def kernel(
    pre_hbm, gh_hbm, qt_hbm, w_hbm, e_hbm, xt_hbm, q_out, gi_out,
    pre, gh, qt, w, e, xt, g, eb, part, ring,
    h_part, h_rs, h_ag, z_part, z_rs, z_ag,
    px_part, px_rs, px_y, pt,
    pe_part, pe_send, pe_c, pe_x, pe_s, pe_z, pf_row, pf, p_wide,
    y_part, y_c, y_x, y_y, y_f, y_err, work,
    s_z, r_z, s_q, r_q, s_x, r_x, s_y, r_y, s_c, r_c, s_g, r_g, s_in,
):
    dp, z = lax.axis_index("dp"), lax.axis_index("tensor")
    c, x, y = lax.rem(dp, 2), lax.rem(dp // 2, NX), dp // (2 * NX)
    o, me = 1 - c, c * NX + x

    def at(yy, xx, cc, zz):
        return ((yy * NX + xx) * 2 + cc, zz)

    axes = {
        "z": (NZ, z, lambda j: at(y, x, c, j), s_z, r_z),
        "x": (NX, x, lambda j: at(y, j, c, z), s_x, r_x),
        "q": (2 * NX, c * NX + x, lambda j: at(y, lax.rem(j, NX), j // NX, z), s_q, r_q),
        "y": (NY, y, lambda j: at(j, x, c, z), s_y, r_y),
    }
    sent = []

    def remote(src, dst, ss, rs, dev):
        return pltpu.make_async_remote_copy(
            src_ref=src, dst_ref=dst, send_sem=ss, recv_sem=rs, device_id=dev, device_id_type=MESH)

    def push(src, dst, ss, rs, dev):
        cp = remote(src, dst, ss, rs, dev)
        cp.start()
        sent.append(cp)

    def start(axis, phase, src, dst):
        n, own, dev, ss, rs = axes[axis]
        for k in FAR[n]:
            j = lax.rem(own + k, n)
            push(src(j), dst(own), ss.at[phase, k], rs.at[phase, own], dev(j))

    def finish(axis, phase, dst):
        n, own, dev, ss, rs = axes[axis]
        for k in FAR[n]:
            j = lax.rem(own + k, n)
            remote(dst(j), dst(j), ss.at[phase, k], rs.at[phase, j], dev(j)).wait_recv()

    def swap(phase, src, dst):
        push(src, dst, s_c.at[phase], r_c.at[phase], at(y, x, o, z))

    def swapped(phase, dst):
        remote(dst, dst, s_c.at[phase], r_c.at[phase], at(y, x, o, z)).wait_recv()

    def shifted(direction, hops):
        return lax.rem(z + (hops if direction == 0 else NZ - hops), NZ)

    def piece(direction, m, ch):
        half = (direction + m) % 2
        return pl.ds(half * HALF + ch * CHUNK, CHUNK)

    def ring_send(direction, m, ch, src):
        push(src, ring.at[direction, m, ch], s_g.at[direction, m, ch], r_g.at[direction, m, ch],
             at(y, x, c, shifted(direction, 1)))

    def ring_wait(direction, m, ch):
        slot = ring.at[direction, m, ch]
        remote(slot, slot, s_g.at[direction, m, ch], r_g.at[direction, m, ch],
               at(y, x, c, shifted(direction, 1))).wait_recv()

    todo = [(m, ch) for m in range(7) for ch in range(NCH)]

    def advance(count):
        for m, ch in todo[:count]:
            for direction in range(2):
                mine = part.at[shifted(direction, HOPS[m]), piece(direction, m, ch)]
                if m < 2:
                    ring_send(direction, m, ch, mine)
                else:
                    ring_wait(direction, m - 2, ch)
                    slot = ring.at[direction, m - 2, ch]
                    slot[...] = (slot[...].astype(F32) + mine[...].astype(F32)).astype(BF16)
                    ring_send(direction, m, ch, slot)
        del todo[:count]

    def product(t):
        rows = w[pl.ds(pl.multiple_of(t * FEAT, FEAT), FEAT), :]
        part[t] = dot(rows, g[...], NT).astype(BF16)

    def drain():
        while sent:
            sent.pop(0).wait_send()

    def load(src, dst, i):
        cp = pltpu.make_async_copy(src, dst, s_in.at[i])
        cp.start()
        return cp

    def block(t):
        return pl.ds(pl.multiple_of(t * FEAT, FEAT), FEAT)

    order = [shifted(0, 4), shifted(0, 3), shifted(1, 3), shifted(0, 2), shifted(1, 2), shifted(0, 1), shifted(1, 1), z]

    def load_w(i):
        return load(w_hbm.at[block(order[i])], w.at[block(order[i])], 4 + i)

    def load_e(t):
        return pltpu.make_async_copy(e_hbm.at[block(t)], e.at[block(t)], s_in.at[12 + t])

    loads = [load(pre_hbm, pre, 0), load(gh_hbm, gh, 1), load(qt_hbm, qt, 2)]
    barrier = pltpu.get_barrier_semaphore()
    for axis in "zyq":
        n, own, dev = axes[axis][:3]
        for k in FAR[n]:
            pl.semaphore_signal(barrier, inc=1, device_id=dev(lax.rem(own + k, n)), device_id_type=MESH)
    eye = (lax.broadcasted_iota(jnp.int32, (R, R), 0) == lax.broadcasted_iota(jnp.int32, (R, R), 1)).astype(F32)

    loads[0].wait()
    loads[1].wait()
    w_loads = [load_w(i) for i in range(3)]
    for t in range(NZ):
        load_e(t).start()
    w_loads += [load_w(i) for i in range(3, NZ)]
    x_load = load(xt_hbm, xt, 3)

    def activate(i, carry):
        rows = pl.ds(pl.multiple_of(i * 32, 32), 32)
        g[rows, :] = (gh[rows, :].astype(F32) * gelu_slope(pre[rows, :].astype(F32))).astype(BF16)
        return carry

    lax.fori_loop(0, TOK // 32, activate, 0)
    loads[2].wait()
    h_part[...] = pair_rows(dot_wide(qt[...], g[...], NT).reshape(NZ, 8, TOK)).astype(BF16)
    pl.semaphore_wait(barrier, 17)
    start("z", 0, lambda j: h_part.at[j], lambda i: h_rs.at[i])
    h_rs[z] = h_part[z]
    w_loads[0].wait()
    product(order[0])
    advance(SENDS["a"])

    def error_rows(t, carry):
        load_e(t).wait()
        eb[block(t), :] = e[block(t), :].astype(BF16)
        pe_part[:, :, t] = dot_wide(qt[...], eb[block(t), :], NT).reshape(2, NX, 8, FEAT)
        return carry

    lax.fori_loop(0, NZ, error_rows, 0)
    pe_send[...] = pe_part[o].reshape(NX, R, FEAT).astype(BF16)
    swap(0, pe_send, pe_c)
    w_loads[1].wait()
    product(order[1])
    w_loads[2].wait()
    product(order[2])
    advance(SENDS["b"])
    swapped(0, pe_c)
    pe_c[...] = (pe_c[...].astype(F32) + pe_part[c].reshape(NX, R, FEAT)).astype(BF16)
    start("x", 0, lambda j: pe_c.at[j], lambda i: pe_x.at[i])
    pe_x[x] = pe_c[x]
    finish("z", 0, lambda i: h_rs.at[i])
    h_ag[z] = jnp.sum(h_rs[...].astype(F32), axis=0).astype(BF16)
    start("z", 1, lambda j: h_ag.at[z], lambda i: h_ag.at[i])
    advance(SENDS["c"])
    for cp in w_loads[3:]:
        cp.wait()

    def products(k, carry):
        product(lax.rem(z + NZ - 2 + k, NZ))
        return carry

    lax.fori_loop(0, 5, products, 0)
    finish("x", 0, lambda i: pe_x.at[i])
    pe_s[...] = jnp.sum(pe_x[...].astype(F32), axis=0).reshape(NZ, 8, FEAT)
    start("z", 2, lambda j: pe_s.at[j], lambda i: pe_z.at[i])
    pe_z[z] = pe_s[z]
    x_load.wait()
    advance(SENDS["d"])
    finish("z", 1, lambda i: h_ag.at[i])
    h_all = unpair_rows(h_ag[...].astype(F32)).reshape(R, TOK).astype(BF16)
    px_part[...] = dot(h_all, xt[...], NT).reshape(2 * NX, 8, FEAT)
    start("q", 0, lambda j: px_part.at[j], lambda i: px_rs.at[i])
    px_rs[me] = px_part[me]
    advance(SENDS["e"])
    advance(SENDS["f"])
    finish("z", 2, lambda i: pe_z.at[i])
    pe_sum = jnp.sum(pe_z[...], axis=0)
    finish("q", 0, lambda i: px_rs.at[i])
    px_y[y] = jnp.sum(px_rs[...], axis=0) + pe_sum
    start("y", 0, lambda j: px_y.at[y], lambda i: px_y.at[i])
    advance(SENDS["g"])
    finish("y", 0, lambda i: px_y.at[i])
    p_row = jnp.sum(px_y[...], axis=0)
    pt[me] = p_row
    pf_row[z] = p_row
    start("q", 1, lambda j: pt.at[me], lambda i: pt.at[i])
    start("z", 3, lambda j: pf_row.at[z], lambda i: pf_row.at[i])
    advance(SENDS["h"])
    finish("q", 1, lambda i: pt.at[i])
    z_sum = dot_wide(pt[...].reshape(R, FEAT), xt[...], NN).reshape(NZ, 8, TOK)
    z_part[...] = pair_rows(z_sum).astype(BF16)
    start("z", 4, lambda j: z_part.at[j], lambda i: z_rs.at[i])
    z_rs[z] = z_part[z]
    advance(SENDS["i"])
    finish("z", 3, lambda i: pf_row.at[i])
    pf[c, x] = pf_row[...].reshape(R, FEAT).astype(BF16)
    start("x", 3, lambda j: pf.at[c, x], lambda i: pf.at[c, i])
    advance(SENDS["j"])
    finish("z", 4, lambda i: z_rs.at[i])
    z_ag[z] = jnp.sum(z_rs[...].astype(F32), axis=0).astype(BF16)
    start("z", 5, lambda j: z_ag.at[z], lambda i: z_ag.at[i])
    advance(SENDS["k"])
    finish("x", 3, lambda i: pf.at[c, i])
    swap(3, pf.at[c], pf.at[c])
    swapped(3, pf.at[o])

    def features(t, carry):
        y_err[...] += dot(p_wide[:, t].reshape(R, FEAT).astype(BF16), eb[block(t), :], NN)
        return carry

    def squares(t, gram):
        rows = p_wide[:, t].reshape(R, FEAT).astype(BF16)
        return gram + dot(rows, rows, NT)

    p_wide[...] = pf[...].astype(F32).reshape(2 * NX, NZ, 8, FEAT)
    y_err[...] = jnp.zeros_like(y_err)
    lax.fori_loop(0, NZ, features, 0)
    advance(SENDS["l"])
    drain()
    finish("z", 5, lambda i: z_ag.at[i])
    z_all = unpair_rows(z_ag[...].astype(F32)).reshape(R, TOK).astype(BF16)
    y_part[...] = (y_err[...] + dot(z_all, g[...], NN)).reshape(2, NX, 8, HID)
    swap(4, y_part.at[o], y_c)
    advance(SENDS["m"])
    swapped(4, y_c)
    y_c[...] += y_part[c]
    start("x", 4, lambda j: y_c.at[j], lambda i: y_x.at[i])
    y_x[x] = y_c[x]
    advance(SENDS["n"])
    gram = lax.fori_loop(0, NZ, squares, jnp.zeros((R, R), F32))
    work[...] = jnp.concatenate([gram, eye], axis=1)
    eliminate(work, 0, 14, z >= 0)
    finish("x", 4, lambda i: y_x.at[i])
    y_y[y] = jnp.sum(y_x[...], axis=0)
    start("y", 1, lambda j: y_y.at[y], lambda i: y_y.at[i])
    advance(SENDS["o"])
    eliminate(work, 14, 36, z >= 0)
    finish("y", 1, lambda i: y_y.at[i])
    y_f[c, x] = jnp.sum(y_y[...], axis=0)
    start("x", 5, lambda j: y_f.at[c, x], lambda i: y_f.at[c, i])
    advance(SENDS["p"])
    eliminate(work, 36, 58, z >= 0)
    finish("x", 5, lambda i: y_f.at[c, i])
    swap(5, y_f.at[c], y_f.at[c])
    advance(SENDS["q"])
    eliminate(work, 58, 64, z >= 0)
    diag = jnp.sum(work[:, :R] * eye, axis=1, keepdims=True)
    inverse = work[:, R:] * (lax.rsqrt(diag) * (1.0 / (NX * NY * 2)))
    advance(len(todo))
    for m in (5, 6):
        for ch in range(NCH):
            for direction in range(2):
                ring_wait(direction, m, ch)
    for half in range(2):
        for ch in range(NCH):
            rows = pl.ds(half * HALF + ch * CHUNK, CHUNK)
            long, short = ring[half, 6, ch].astype(F32), ring[1 - half, 5, ch].astype(F32)
            gi_out[rows, :] = (part[z, rows].astype(F32) + long + short).astype(BF16)
    swapped(5, y_f.at[o])
    q_out[...] = dot_both(inverse, y_f[...].reshape(R, HID), NN)
    drain()


def local(tokens, w_in, pre_act, grad_hidden, err_state, q_init):
    vm = lambda *shape: pltpu.VMEM(shape, F32)
    vb = lambda *shape: pltpu.VMEM(shape, BF16)
    dma = pltpu.SemaphoreType.DMA
    q_factor, grad_input = pl.pallas_call(
        kernel,
        out_shape=[vm(R, HID), vb(FEAT, TOK)],
        in_specs=[pl.BlockSpec(memory_space=pl.ANY)] * 6,
        out_specs=[pl.BlockSpec(memory_space=pltpu.VMEM)] * 2,
        scratch_shapes=[vb(TOK, HID), vb(TOK, HID), vm(R, HID), vb(NZ * FEAT, HID), vm(NZ * FEAT, HID),
                        vb(FEAT, TOK), vb(TOK, HID), vb(NZ * FEAT, HID), vb(NZ, FEAT, TOK), vb(2, 7, NCH, CHUNK, TOK)]
        + [vb(NZ, 16, TOK // 2)] * 6
        + [vm(2 * NX, 8, FEAT), vm(2 * NX, 8, FEAT), vm(NY, 8, FEAT), vm(2 * NX, 8, FEAT)]
        + [vm(2, NX, NZ, 8, FEAT), vb(NX, R, FEAT), vb(NX, R, FEAT), vb(NX, R, FEAT), vm(NZ, 8, FEAT), vm(NZ, 8, FEAT),
           vm(NZ, 8, FEAT), vb(2, NX, R, FEAT), vm(2 * NX, NZ, 8, FEAT)]
        + [vm(2, NX, 8, HID), vm(NX, 8, HID), vm(NX, 8, HID), vm(NY, 8, HID), vm(2, NX, 8, HID), vm(R, HID),
           vm(R, 2 * R)]
        + [dma((6, NZ)), dma((6, NZ)), dma((2, 2 * NX)), dma((2, 2 * NX)), dma((6, NX)), dma((6, NX)), dma((2, NY)), dma((2, NY)), dma((6,)), dma((6,)),
           dma((2, 7, NCH)), dma((2, 7, NCH)), dma((20,))],
        compiler_params=pltpu.CompilerParams(
            collective_id=0, has_side_effects=True, vmem_limit_bytes=56 << 20),
        name="backward",
    )(pre_act, grad_hidden, q_init.T, w_in, err_state[0], tokens.T)
    return (grad_input.T, q_factor.T)


def solution(mesh):
    return jax.shard_map(
        local,
        mesh=mesh,
        in_specs=(
            P("dp", "tensor"),
            P(None, "tensor"),
            P("dp", "tensor"),
            P("dp", "tensor"),
            P("dp", None, "tensor"),
            P("tensor", None),
        ),
        out_specs=(P("dp", "tensor"), P("tensor", None)),
        check_vma=False,
    )
```

```python
import jax
import jax.numpy as jnp
from jax import lax
from jax.experimental import pallas as pl
from jax.experimental.pallas import tpu as pltpu
from jax.sharding import PartitionSpec as P

slope_coeff = 0.7978845608
MESH = pl.DeviceIdType.MESH
F32, BF16 = jnp.float32, jnp.bfloat16
NX, NY, NZ = 4, 4, 8
R, TOK, FEAT, HID = 64, 768, 320, 640
NCH = 2
HALF = FEAT // 2
CHUNK = HALF // NCH
HOPS = (4, 3, 3, 2, 2, 1, 1)
SENDS = dict(a=2, b=0, c=0, d=1, e=1, f=1, g=1, h=1, i=1, j=0, k=1, l=0, m=4, n=1, o=0, p=0, q=0)
FAR = {4: (2, 1, 3), 8: (4, 3, 5, 2, 6, 1, 7)}
NN = (((1,), (0,)), ((), ()))
NT = (((1,), (1,)), ((), ()))


def gelu_slope(argument):
    square = argument * argument
    tangent = jnp.tanh(argument * (slope_coeff + (slope_coeff * 0.044715) * square))
    linear = argument * (slope_coeff + (slope_coeff * 0.134145) * square)
    return 0.5 * (1.0 + tangent) * (1.0 + (1.0 - tangent) * linear)


def halves(value):
    high = value.astype(BF16)
    return high, (value - high.astype(F32)).astype(BF16)


def dot(left, right, dims):
    return lax.dot_general(left, right, dims, preferred_element_type=F32)


def dot_wide(left, right, dims):
    rows = left.shape[0]
    both = dot(jnp.concatenate(halves(left), axis=0), right, dims)
    return both[:rows] + both[rows:]


def pair_rows(value):
    n = value.shape[-1] // 2
    return jnp.concatenate([value[..., :n], value[..., n:]], axis=-2)


def unpair_rows(value):
    return jnp.concatenate([value[..., :8, :], value[..., 8:, :]], axis=-1)


def eliminate(work, first, last, here):
    @pl.when(here)
    def _():
        whole = work[...]
        below = lax.broadcasted_iota(jnp.int32, (R, 1), 0)
        for k in range(first, last):
            row = whole[k:k + 1, :]
            column = whole[:, k:k + 1]
            ratio = jnp.where(below > k, column / whole[k:k + 1, k:k + 1], 0.0)
            whole = whole - ratio * row
        work[...] = whole


def kernel(
    pre_hbm, gh_hbm, qt_hbm, w_hbm, e_hbm, xt_hbm, q_out, gi_out,
    pre, gh, qt, w, e, xt, g, eb, part, ring,
    h_part, h_rs, h_ag, z_part, z_rs, z_ag,
    px_part, px_rs, px_y, pt,
    pe_part, pe_send, pe_c, pe_x, pe_s, pe_z, pf_row, pf, p_wide,
    y_part, y_rs, y_y, y_f, y_err, work,
    s_z, r_z, s_q, r_q, s_x, r_x, s_y, r_y, s_c, r_c, s_g, r_g, s_in,
):
    dp, z = lax.axis_index("dp"), lax.axis_index("tensor")
    c, x, y = lax.rem(dp, 2), lax.rem(dp // 2, NX), dp // (2 * NX)
    o, me = 1 - c, c * NX + x

    def at(yy, xx, cc, zz):
        return ((yy * NX + xx) * 2 + cc, zz)

    axes = {
        "z": (NZ, z, lambda j: at(y, x, c, j), s_z, r_z),
        "x": (NX, x, lambda j: at(y, j, c, z), s_x, r_x),
        "q": (2 * NX, c * NX + x, lambda j: at(y, lax.rem(j, NX), j // NX, z), s_q, r_q),
        "y": (NY, y, lambda j: at(j, x, c, z), s_y, r_y),
    }
    sent = []

    def remote(src, dst, ss, rs, dev):
        return pltpu.make_async_remote_copy(
            src_ref=src, dst_ref=dst, send_sem=ss, recv_sem=rs, device_id=dev, device_id_type=MESH)

    def push(src, dst, ss, rs, dev):
        cp = remote(src, dst, ss, rs, dev)
        cp.start()
        sent.append(cp)

    def start(axis, phase, src, dst):
        n, own, dev, ss, rs = axes[axis]
        for k in FAR[n]:
            j = lax.rem(own + k, n)
            push(src(j), dst(own), ss.at[phase, k], rs.at[phase, own], dev(j))

    def finish(axis, phase, dst):
        n, own, dev, ss, rs = axes[axis]
        for k in FAR[n]:
            j = lax.rem(own + k, n)
            remote(dst(j), dst(j), ss.at[phase, k], rs.at[phase, j], dev(j)).wait_recv()

    def swap(phase, src, dst):
        push(src, dst, s_c.at[phase], r_c.at[phase], at(y, x, o, z))

    def swapped(phase, dst):
        remote(dst, dst, s_c.at[phase], r_c.at[phase], at(y, x, o, z)).wait_recv()

    def shifted(direction, hops):
        return lax.rem(z + (hops if direction == 0 else NZ - hops), NZ)

    def piece(direction, m, ch):
        half = (direction + m) % 2
        return pl.ds(half * HALF + ch * CHUNK, CHUNK)

    def ring_send(direction, m, ch, src):
        push(src, ring.at[direction, m, ch], s_g.at[direction, m, ch], r_g.at[direction, m, ch],
             at(y, x, c, shifted(direction, 1)))

    def ring_wait(direction, m, ch):
        slot = ring.at[direction, m, ch]
        remote(slot, slot, s_g.at[direction, m, ch], r_g.at[direction, m, ch],
               at(y, x, c, shifted(direction, 1))).wait_recv()

    todo = [(m, ch) for m in range(7) for ch in range(NCH)]

    def advance(count):
        for m, ch in todo[:count]:
            for direction in range(2):
                mine = part.at[shifted(direction, HOPS[m]), piece(direction, m, ch)]
                if m < 2:
                    ring_send(direction, m, ch, mine)
                else:
                    ring_wait(direction, m - 2, ch)
                    slot = ring.at[direction, m - 2, ch]
                    slot[...] = (slot[...].astype(F32) + mine[...].astype(F32)).astype(BF16)
                    ring_send(direction, m, ch, slot)
        del todo[:count]

    def product(t):
        rows = w[pl.ds(pl.multiple_of(t * FEAT, FEAT), FEAT), :]
        part[t] = dot(rows, g[...], NT).astype(BF16)

    def drain():
        while sent:
            sent.pop(0).wait_send()

    def load(src, dst, i):
        cp = pltpu.make_async_copy(src, dst, s_in.at[i])
        cp.start()
        return cp

    def block(t):
        return pl.ds(pl.multiple_of(t * FEAT, FEAT), FEAT)

    order = [shifted(0, 4), shifted(0, 3), shifted(1, 3), shifted(0, 2), shifted(1, 2), shifted(0, 1), shifted(1, 1), z]

    def load_w(i):
        return load(w_hbm.at[block(order[i])], w.at[block(order[i])], 4 + i)

    def load_e(t):
        return pltpu.make_async_copy(e_hbm.at[block(t)], e.at[block(t)], s_in.at[12 + t])

    barrier = pltpu.get_barrier_semaphore()
    for axis in "zyq":
        n, own, dev = axes[axis][:3]
        for k in FAR[n]:
            pl.semaphore_signal(barrier, inc=1, device_id=dev(lax.rem(own + k, n)), device_id_type=MESH)
    loads = [load(pre_hbm, pre, 0), load(gh_hbm, gh, 1), load(qt_hbm, qt, 2)]
    eye = (lax.broadcasted_iota(jnp.int32, (R, R), 0) == lax.broadcasted_iota(jnp.int32, (R, R), 1)).astype(F32)

    loads[0].wait()
    loads[1].wait()
    w_loads = [load_w(i) for i in range(3)]
    for t in range(NZ):
        load_e(t).start()
    w_loads += [load_w(i) for i in range(3, NZ)]
    x_load = load(xt_hbm, xt, 3)

    def activate(i, carry):
        rows = pl.ds(pl.multiple_of(i * 32, 32), 32)
        g[rows, :] = (gh[rows, :].astype(F32) * gelu_slope(pre[rows, :].astype(F32))).astype(BF16)
        return carry

    lax.fori_loop(0, TOK // 32, activate, 0)
    loads[2].wait()
    h_part[...] = pair_rows(dot_wide(qt[...], g[...], NT).reshape(NZ, 8, TOK)).astype(BF16)
    w_loads[0].wait()
    product(order[0])
    pl.semaphore_wait(barrier, 17)
    start("z", 0, lambda j: h_part.at[j], lambda i: h_rs.at[i])
    h_rs[z] = h_part[z]
    advance(SENDS["a"])

    def error_rows(t, carry):
        load_e(t).wait()
        eb[block(t), :] = e[block(t), :].astype(BF16)
        pe_part[:, :, t] = dot_wide(qt[...], eb[block(t), :], NT).reshape(2, NX, 8, FEAT)
        return carry

    lax.fori_loop(0, NZ, error_rows, 0)
    pe_send[...] = pe_part[o].reshape(NX, R, FEAT).astype(BF16)
    swap(0, pe_send, pe_c)
    w_loads[1].wait()
    product(order[1])
    w_loads[2].wait()
    product(order[2])
    advance(SENDS["b"])
    swapped(0, pe_c)
    pe_c[...] = (pe_c[...].astype(F32) + pe_part[c].reshape(NX, R, FEAT)).astype(BF16)
    start("x", 0, lambda j: pe_c.at[j], lambda i: pe_x.at[i])
    pe_x[x] = pe_c[x]
    finish("z", 0, lambda i: h_rs.at[i])
    h_ag[z] = jnp.sum(h_rs[...].astype(F32), axis=0).astype(BF16)
    start("z", 1, lambda j: h_ag.at[z], lambda i: h_ag.at[i])
    advance(SENDS["c"])
    for cp in w_loads[3:]:
        cp.wait()

    def products(k, carry):
        product(lax.rem(z + NZ - 2 + k, NZ))
        return carry

    lax.fori_loop(0, 5, products, 0)
    finish("x", 0, lambda i: pe_x.at[i])
    pe_s[...] = pair_rows(jnp.sum(pe_x[...].astype(F32), axis=0).reshape(NZ, 8, FEAT)).astype(BF16)
    start("z", 2, lambda j: pe_s.at[j], lambda i: pe_z.at[i])
    pe_z[z] = pe_s[z]
    x_load.wait()
    advance(SENDS["d"])
    finish("z", 1, lambda i: h_ag.at[i])
    h_all = unpair_rows(h_ag[...].astype(F32)).reshape(R, TOK).astype(BF16)
    px_part[...] = dot(h_all, xt[...], NT).reshape(2 * NX, 8, FEAT)
    start("q", 0, lambda j: px_part.at[j], lambda i: px_rs.at[i])
    px_rs[me] = px_part[me]
    advance(SENDS["e"])
    advance(SENDS["f"])
    finish("z", 2, lambda i: pe_z.at[i])
    pe_sum = unpair_rows(jnp.sum(pe_z[...].astype(F32), axis=0))
    finish("q", 0, lambda i: px_rs.at[i])
    px_y[y] = jnp.sum(px_rs[...], axis=0) + pe_sum
    start("y", 0, lambda j: px_y.at[y], lambda i: px_y.at[i])
    advance(SENDS["g"])
    finish("y", 0, lambda i: px_y.at[i])
    p_row = jnp.sum(px_y[...], axis=0)
    pt[me] = p_row
    pf_row[z] = pair_rows(p_row).astype(BF16)
    start("q", 1, lambda j: pt.at[me], lambda i: pt.at[i])
    start("z", 3, lambda j: pf_row.at[z], lambda i: pf_row.at[i])
    advance(SENDS["h"])
    finish("q", 1, lambda i: pt.at[i])
    z_sum = dot_wide(pt[...].reshape(R, FEAT), xt[...], NN).reshape(NZ, 8, TOK)
    z_part[...] = pair_rows(z_sum).astype(BF16)
    start("z", 4, lambda j: z_part.at[j], lambda i: z_rs.at[i])
    z_rs[z] = z_part[z]
    advance(SENDS["i"])
    finish("z", 3, lambda i: pf_row.at[i])
    pf[c, x] = unpair_rows(pf_row[...].astype(F32)).reshape(R, FEAT).astype(BF16)
    start("x", 3, lambda j: pf.at[c, x], lambda i: pf.at[c, i])
    advance(SENDS["j"])
    finish("z", 4, lambda i: z_rs.at[i])
    z_ag[z] = jnp.sum(z_rs[...].astype(F32), axis=0).astype(BF16)
    start("z", 5, lambda j: z_ag.at[z], lambda i: z_ag.at[i])
    advance(SENDS["k"])
    finish("x", 3, lambda i: pf.at[c, i])
    swap(3, pf.at[c], pf.at[c])
    swapped(3, pf.at[o])

    def features(t, carry):
        y_err[...] += dot(p_wide[:, t].reshape(R, FEAT).astype(BF16), eb[block(t), :], NN)
        return carry

    def squares(t, gram):
        rows = p_wide[:, t].reshape(R, FEAT).astype(BF16)
        return gram + dot(rows, rows, NT)

    p_wide[...] = pf[...].astype(F32).reshape(2 * NX, NZ, 8, FEAT)
    y_err[...] = jnp.zeros_like(y_err)
    lax.fori_loop(0, NZ, features, 0)
    advance(SENDS["l"])
    drain()
    finish("z", 5, lambda i: z_ag.at[i])
    z_all = unpair_rows(z_ag[...].astype(F32)).reshape(R, TOK).astype(BF16)
    y_sum = (y_err[...] + dot(z_all, g[...], NN)).reshape(2 * NX, 8, HID)
    y_part[...] = pair_rows(y_sum).astype(BF16)
    start("q", 2, lambda j: y_part.at[j], lambda i: y_rs.at[i])
    y_rs[me] = y_part[me]
    advance(SENDS["m"])
    gram = lax.fori_loop(0, NZ, squares, jnp.zeros((R, R), F32))
    work[...] = jnp.concatenate([gram, eye], axis=1)
    eliminate(work, 0, 18, z >= 0)
    finish("q", 2, lambda i: y_rs.at[i])
    y_y[y] = jnp.sum(y_rs[...].astype(F32), axis=0).astype(BF16)
    start("y", 1, lambda j: y_y.at[y], lambda i: y_y.at[i])
    advance(SENDS["n"])
    advance(SENDS["o"])
    eliminate(work, 18, 40, z >= 0)
    finish("y", 1, lambda i: y_y.at[i])
    y_f[me] = jnp.sum(y_y[...].astype(F32), axis=0).astype(BF16)
    start("q", 3, lambda j: y_f.at[me], lambda i: y_f.at[i])
    advance(SENDS["p"])
    advance(SENDS["q"])
    eliminate(work, 40, 64, z >= 0)
    diag = jnp.sum(work[:, :R] * eye, axis=1, keepdims=True)
    inverse = work[:, R:] * (lax.rsqrt(diag) * (1.0 / (NX * NY * 2)))
    advance(len(todo))
    for m in (5, 6):
        for ch in range(NCH):
            for direction in range(2):
                ring_wait(direction, m, ch)
    for half in range(2):
        for ch in range(NCH):
            rows = pl.ds(half * HALF + ch * CHUNK, CHUNK)
            long, short = ring[half, 6, ch].astype(F32), ring[1 - half, 5, ch].astype(F32)
            gi_out[rows, :] = (part[z, rows].astype(F32) + long + short).astype(BF16)
    finish("q", 3, lambda i: y_f.at[i])
    y_all = unpair_rows(y_f[...].astype(F32)).reshape(R, HID).astype(BF16)
    q_out[...] = dot_wide(inverse, y_all, NN)
    drain()


def local(tokens, w_in, pre_act, grad_hidden, err_state, q_init):
    vm = lambda *shape: pltpu.VMEM(shape, F32)
    vb = lambda *shape: pltpu.VMEM(shape, BF16)
    dma = pltpu.SemaphoreType.DMA
    q_factor, grad_input = pl.pallas_call(
        kernel,
        out_shape=[vm(R, HID), vb(FEAT, TOK)],
        in_specs=[pl.BlockSpec(memory_space=pl.ANY)] * 6,
        out_specs=[pl.BlockSpec(memory_space=pltpu.VMEM)] * 2,
        scratch_shapes=[vb(TOK, HID), vb(TOK, HID), vm(R, HID), vb(NZ * FEAT, HID), vm(NZ * FEAT, HID),
                        vb(FEAT, TOK), vb(TOK, HID), vb(NZ * FEAT, HID), vb(NZ, FEAT, TOK), vb(2, 7, NCH, CHUNK, TOK)]
        + [vb(NZ, 16, TOK // 2)] * 6
        + [vm(2 * NX, 8, FEAT), vm(2 * NX, 8, FEAT), vm(NY, 8, FEAT), vm(2 * NX, 8, FEAT)]
        + [vm(2, NX, NZ, 8, FEAT), vb(NX, R, FEAT), vb(NX, R, FEAT), vb(NX, R, FEAT), vb(NZ, 16, FEAT // 2), vb(NZ, 16, FEAT // 2),
           vb(NZ, 16, FEAT // 2), vb(2, NX, R, FEAT), vm(2 * NX, NZ, 8, FEAT)]
        + [vb(2 * NX, 16, HID // 2), vb(2 * NX, 16, HID // 2), vb(NY, 16, HID // 2), vb(2 * NX, 16, HID // 2), vm(R, HID),
           vm(R, 2 * R)]
        + [dma((6, NZ)), dma((6, NZ)), dma((4, 2 * NX)), dma((4, 2 * NX)), dma((6, NX)), dma((6, NX)), dma((2, NY)), dma((2, NY)), dma((6,)), dma((6,)),
           dma((2, 7, NCH)), dma((2, 7, NCH)), dma((20,))],
        compiler_params=pltpu.CompilerParams(
            collective_id=0, has_side_effects=True, vmem_limit_bytes=56 << 20),
        name="backward",
    )(pre_act, grad_hidden, q_init.T, w_in, err_state[0], tokens.T)
    return (grad_input.T, q_factor.T)


def solution(mesh):
    return jax.shard_map(
        local,
        mesh=mesh,
        in_specs=(
            P("dp", "tensor"),
            P(None, "tensor"),
            P("dp", "tensor"),
            P("dp", "tensor"),
            P("dp", None, "tensor"),
            P("tensor", None),
        ),
        out_specs=(P("dp", "tensor"), P("tensor", None)),
        check_vma=False,
    )
```
